32 devices in a mesh: dp: 2 (over x), ctx: 4 (over z), space: 4 (over y, core).
Axes of the slice: x: 2, y: 2, z: 4, core: 2. Of those that a mesh axis runs over, the one named last changes fastest.
Arguments:
- inputs: bfloat16 [8, 4, 256, 3072], P('dp', 'ctx', 'space'), may hold values from -64 to 64
- upstream: bfloat16 [8, 4, 256, 3072], P('dp', 'ctx', 'space'), may hold values from -6 to 6
- qkv_weight: bfloat16 [3, 3072, 1536], P(None, None, 'space'), may hold values from -0.109375 to 0.109375
- out_weight: bfloat16 [3072, 1536], P(None, 'space'), may hold values from -0.15625 to 0.15625
Outputs:
- input_grad: bfloat16 [8, 4, 256, 3072], P('dp', 'ctx', 'space')
- qkv_grad: float32 [3, 3072, 1536], P(None, ('dp', 'ctx'), 'space')
- proj_grad: float32 [3072, 1536], P(('dp', 'ctx'), 'space')
The draws below stay inside these ranges and needn't reach their ends.
All inputs are finite; a program needn't handle non-finite values.
Results may differ from the reference program's by a relative error of at most 0.01.
The reference program's roundings to bfloat16 on the way count: a program that leaves them out, or rounds other values in their place, can miss the bound.
Values may be sent and summed in bfloat16 or wider, within the bound.
No kernel may reach another device: no remote copies, remote signals or barrier semaphores. Data moves between devices by JAX's collectives and lax.ppermute only.
A program may use at most 192 MiB of HBM per device.

```python
import math
import jax
import jax.numpy as jnp
from jax import lax

D = 3072
HEADS = 12
HS = 128
CLIPS = 8
FRAMES = 4
PATCHES = 256
E = 1536
N_SPACE = 4


def draw_inputs(key, part):
    key_base = jax.random.fold_in(jax.random.fold_in(key, 17), 0)
    shape = (CLIPS, FRAMES, PATCHES, D)
    values = jnp.clip(jax.random.normal(key_base, shape, jnp.float32), -6.0, 6.0)
    return jnp.clip(values, -64.0, 64.0).astype(jnp.bfloat16)


def spiked(values, rng, source, target, shards_of, factor):
    owner, partner = [(jnp.arange(values.shape[position]) // (values.shape[position] // shards_of)).reshape([-1 if axis == position else 1 for axis in range(values.ndim)]) for position in (source, target)]
    chosen = jax.random.permutation(rng, shards_of)[partner]
    strong = (owner == chosen) | (owner == (partner + shards_of // 2) % shards_of)
    return jnp.where(strong, factor * values, values)


def block_levels(stream_key, extent, pieces, low, high):
    level, own = 1.0, jax.random.fold_in(stream_key, 6)
    for position, parts in pieces:
        steps = jnp.exp(jax.random.uniform(jax.random.fold_in(own, position), (parts,), jnp.float32, low / len(pieces), high / len(pieces)))
        level = level * jnp.repeat(steps, extent[position] // parts).reshape([-1 if axis == position else 1 for axis in range(len(extent))])
    return level


def gaussian(key, shape, scale, most, cuts=(), dtype=jnp.bfloat16):
    level = block_levels(key, shape, cuts, -0.22, 0.18) if cuts else 1.0
    values = jax.random.normal(key, shape, jnp.float32) * scale * level
    return jnp.minimum(jnp.maximum(values, -most), most).astype(dtype)


def noise_with(own_key, extent, deviation, most, pieces, heavy, held_as=jnp.bfloat16):
    result = deviation * jax.random.normal(own_key, extent, jnp.float32)
    if pieces:
        result = result * block_levels(own_key, extent, pieces, -0.22, 0.18)
    return jnp.clip(spiked(result, jax.random.fold_in(own_key, 3), *heavy), -most, most).astype(held_as)


def setup_inputs(seed: int = 0) -> dict:
    key_of = jax.random.split(jax.random.key(seed), 5)
    return {
        "inputs": draw_inputs(jax.random.fold_in(key_of[4], 71), 0),
        "upstream": noise_with(key_of[1], (CLIPS, FRAMES, PATCHES, D), 1.0, 6.0, ((0, 2), (1, 4), (2, 4)), (1, 3, 4, 2.0)),
        "qkv_weight": gaussian(key_of[2], (3, D, E), D ** -0.5, 0.109375, ((2, 4),)),
        "out_weight": gaussian(key_of[3], (D, E), E ** -0.5, 0.15625, ((1, 4),)),
    }


def attend_clip(queries, key_rows, value_rows, out_front):
    frames = queries.shape[0]
    scale = 1.0 / math.sqrt(HS)

    def heads_view(array):
        return array.reshape(frames, array.shape[1], HEADS, HS).astype(jnp.float32)
    query_f = heads_view(queries)
    key_f = heads_view(key_rows)
    value_f = heads_view(value_rows)
    front_f = heads_view(out_front)
    scores = jnp.einsum('fphd,gphd->phfg', query_f, key_f) * scale
    causal = jnp.arange(frames)[:, None] >= jnp.arange(frames)[None, :]
    masked = jnp.where(causal, scores, jnp.float32(-1e+30))
    top = lax.optimization_barrier(jnp.max(masked, axis=-1, keepdims=True))
    expo = jnp.where(causal, jnp.exp(masked - top), jnp.float32(0.0))
    probs = expo / lax.optimization_barrier(jnp.sum(expo, axis=-1, keepdims=True))
    probs_b = probs.astype(jnp.bfloat16).astype(jnp.float32)
    attended = jnp.einsum('phfg,gphd->fphd', probs_b, value_f).astype(jnp.bfloat16)
    dprobs = jnp.einsum('fphd,gphd->phfg', front_f, value_f)
    dvalue = jnp.einsum('phfg,fphd->gphd', probs_b, front_f).astype(jnp.bfloat16)
    dscore = probs * (dprobs - lax.optimization_barrier(jnp.sum(probs * dprobs, axis=-1, keepdims=True)))
    dscore_b = dscore.astype(jnp.bfloat16).astype(jnp.float32)
    dquery = (jnp.einsum('phfg,gphd->fphd', dscore_b, key_f) * scale).astype(jnp.bfloat16)
    dkey = (jnp.einsum('phfg,fphd->gphd', dscore_b, query_f) * scale).astype(jnp.bfloat16)
    width = HEADS * HS
    shape = (frames, queries.shape[1], width)
    return (attended.reshape(shape), dquery.reshape(shape), dkey.reshape(shape), dvalue.reshape(shape))

def reference(inputs, upstream, qkv_weight, out_weight):
    width = HEADS * HS
    group = width // N_SPACE

    def one_clip(carry, pair):
        qkv_acc, proj_acc = carry
        clip_in, clip_up = pair
        frames, patches, model = clip_in.shape
        rows = clip_in.reshape(frames * patches, model)
        up_rows = clip_up.reshape(frames * patches, model)
        projected = [jnp.dot(rows, qkv_weight[s], preferred_element_type=jnp.float32).astype(jnp.bfloat16).reshape(frames, patches, width) for s in range(3)]
        out_front = jnp.dot(up_rows, out_weight, preferred_element_type=jnp.float32).astype(jnp.bfloat16).reshape(frames, patches, width)
        attended, dquery, dkey, dvalue = attend_clip(projected[0], projected[1], projected[2], out_front)
        grads = [dquery.reshape(-1, width), dkey.reshape(-1, width), dvalue.reshape(-1, width)]
        proj_acc = proj_acc + jnp.dot(up_rows.T, attended.reshape(-1, width), preferred_element_type=jnp.float32)
        qkv_acc = qkv_acc + jnp.stack([jnp.dot(rows.T, grads[s], preferred_element_type=jnp.float32) for s in range(3)])
        partial_value = jnp.zeros((N_SPACE, frames * patches, model), jnp.float32)
        for s in range(3):
            grad_g = grads[s].reshape(-1, N_SPACE, group).astype(jnp.float32)
            weight_g = qkv_weight[s].reshape(model, N_SPACE, group).astype(jnp.float32)
            partial_value = partial_value + jnp.einsum('tne,dne->ntd', grad_g, weight_g)
        rounded = lax.optimization_barrier(partial_value.astype(jnp.bfloat16)).astype(jnp.float32)
        clip_grad = lax.optimization_barrier(jnp.sum(rounded, axis=0)).astype(jnp.bfloat16).reshape(frames, patches, model)
        return ((qkv_acc, proj_acc), clip_grad)
    start = (jnp.zeros((3, D, width), jnp.float32), jnp.zeros((D, width), jnp.float32))
    (qkv_grad, proj_grad), input_grad = lax.scan(one_clip, start, (inputs, upstream))
    return (input_grad, qkv_grad, proj_grad)
```

```python
import functools
import math

import jax
import jax.numpy as jnp
from jax import lax
from jax.experimental import pallas as pl
from jax.experimental.pallas import tpu as pltpu
from jax.sharding import PartitionSpec as P

HS = 128
F32 = jnp.float32
BF16 = jnp.bfloat16


def attention_kernel(frames, heads, me_ref, q_ref, k_ref, v_ref, o_ref, att_ref, dq_ref, dk_ref, dv_ref):
    me = me_ref[0]
    scale = 1.0 / math.sqrt(HS)
    slots = [lax.rem(me - f + frames, frames) for f in range(frames)]

    for h in range(heads):
        cols = pl.ds(h * HS, HS)

        def load(ref):
            return [ref[0, slots[f], :, cols].astype(F32) for f in range(frames)]

        q, k, v, o = load(q_ref), load(k_ref), load(v_ref), load(o_ref)
        dk = [None] * frames
        dv = [None] * frames
        for f in range(frames):
            scores = [jnp.sum(q[f] * k[g], axis=-1, keepdims=True) * scale for g in range(f + 1)]
            top = functools.reduce(jnp.maximum, scores)
            expo = [jnp.exp(s - top) for s in scores]
            total = functools.reduce(jnp.add, expo)
            probs = [e / total for e in expo]
            probs_b = [p.astype(BF16).astype(F32) for p in probs]
            dprobs = [jnp.sum(o[f] * v[g], axis=-1, keepdims=True) for g in range(f + 1)]
            inner = functools.reduce(jnp.add, [p * d for p, d in zip(probs, dprobs)])
            dscores = [
                (p * (d - inner)).astype(BF16).astype(F32) for p, d in zip(probs, dprobs)
            ]
            att = functools.reduce(jnp.add, [probs_b[g] * v[g] for g in range(f + 1)])
            dq = functools.reduce(jnp.add, [dscores[g] * k[g] for g in range(f + 1)])
            att_ref[0, slots[f], :, cols] = att.astype(BF16)
            dq_ref[0, slots[f], :, cols] = (dq * scale).astype(BF16)
            for g in range(f + 1):
                add_k, add_v = dscores[g] * q[f], probs_b[g] * o[f]
                dk[g] = add_k if dk[g] is None else dk[g] + add_k
                dv[g] = add_v if dv[g] is None else dv[g] + add_v
        for g in range(frames):
            dk_ref[0, slots[g], :, cols] = (dk[g] * scale).astype(BF16)
            dv_ref[0, slots[g], :, cols] = dv[g].astype(BF16)


def attend(me, q, k, v, o):
    groups, frames, patches, width = q.shape
    block = pl.BlockSpec((1, frames, patches, width), lambda i, me_ref: (i, 0, 0, 0))
    return pl.pallas_call(
        functools.partial(attention_kernel, frames, width // HS),
        grid_spec=pltpu.PrefetchScalarGridSpec(
            num_scalar_prefetch=1,
            grid=(groups,),
            in_specs=[block] * 4,
            out_specs=[block] * 4,
        ),
        out_shape=[jax.ShapeDtypeStruct(q.shape, BF16)] * 4,
        compiler_params=pltpu.CompilerParams(vmem_limit_bytes=32 * 1024 * 1024),
        cost_estimate=pl.CostEstimate(
            flops=q.size * 80, bytes_accessed=q.size * 16, transcendentals=q.size * 4
        ),
    )(me.reshape(1), q, k, v, o)


def dot(a, b, contract):
    return lax.dot_general(a, b, ((contract[:1], contract[1:]), ((), ())), preferred_element_type=F32)


def body(sizes, inputs, upstream, qkv_weight, out_weight):
    n_dp, n, n_space = sizes
    me = lax.axis_index("ctx")
    me_dp = lax.axis_index("dp")
    clips, single, patches, model = inputs.shape
    width = qkv_weight.shape[2]
    rows = clips * single * patches // n
    parts = 2
    half = rows // parts
    bits = []
    bit = n_space // 2
    while bit:
        bits.append(bit)
        bit //= 2

    def shift(x, d):
        return lax.ppermute(x, "ctx", [(i, (i + d) % n) for i in range(n)])

    def flip(x, bit):
        return lax.ppermute(x, "space", [(i, i ^ bit) for i in range(n_space)])

    def spread(x, c):
        x = x.reshape(n, rows, model)[:, c * half : (c + 1) * half]

        def to(d):
            return lax.dynamic_index_in_dim(x, lax.rem(me + d, n), 0, keepdims=False)

        own = jnp.stack([to(0)] + [shift(to(d), d) for d in range(1, n)])
        held = [own]
        for bit in bits:
            held = held + [flip(h, bit) for h in held]
        return jnp.stack(held).reshape(-1, model)

    def project(tokens, weight):
        return dot(tokens, weight, (1, 0)).astype(BF16).reshape(n_space, n, half, width)

    tokens = [spread(inputs, c) for c in range(parts)]
    ups = [spread(upstream, c) for c in range(parts)]
    results = []
    for c in range(parts):
        q, k, v = (project(tokens[c], qkv_weight[s]) for s in range(3))
        o = project(ups[c], out_weight)
        results.append(attend(me, q, k, v, o))

    pieces = []
    for c in range(parts):
        _, dq, dk, dv = (r.reshape(-1, width) for r in results[c])
        part = dot(dq, qkv_weight[0], (1, 1)) + dot(dk, qkv_weight[1], (1, 1))
        part = (part + dot(dv, qkv_weight[2], (1, 1))).astype(BF16)
        part = part.reshape(n_space, n, half, model)
        for bit in reversed(bits):
            size = part.shape[0] // 2
            got = flip(part[size:], bit)
            part = (part[:size].astype(F32) + got.astype(F32)).astype(BF16)
        part = part[0]
        back = [part[0]] + [shift(part[d], n - d) for d in range(1, n)]
        back = jnp.stack([back[d] for d in range(n)])
        order = lax.rem(jnp.arange(n) - me + n, n)
        pieces.append(jnp.take(back, order, axis=0))
    input_grad = jnp.stack(pieces, axis=1).reshape(inputs.shape)

    token_all = jnp.concatenate(tokens, 0)
    up_all = jnp.concatenate(ups, 0)

    def reduce_rows(left, right):
        share = model // n_dp
        other = lax.dynamic_slice_in_dim(left, (1 - me_dp) * share, share, 1)
        mine = lax.dynamic_slice_in_dim(left, me_dp * share, share, 1)
        sent = lax.ppermute(dot(other, right, (0, 0)).astype(BF16), "dp", [(0, 1), (1, 0)])
        acc = dot(mine, right, (0, 0)) + sent.astype(F32)
        acc = acc.reshape(n, share // n, width)
        for step in range(n - 1):
            count = n - 1 - step
            start = jnp.where(me == step, step + 1, 0)
            give = lax.dynamic_slice_in_dim(acc, start, count, 0).astype(BF16)
            got = lax.ppermute(give, "ctx", [(step, step + 1), (n - 1 - step, n - 2 - step)])
            at = jnp.where(me == step + 1, step + 1, 0)
            old = lax.dynamic_slice_in_dim(acc, at, count, 0)
            acc = lax.dynamic_update_slice_in_dim(acc, old + got.astype(F32), at, 0)
        return lax.dynamic_index_in_dim(acc, me, 0, keepdims=False)

    cat = [jnp.concatenate([results[c][i].reshape(-1, width) for c in range(parts)], 0) for i in range(4)]
    proj_grad = reduce_rows(up_all, cat[0])
    qkv_grad = jnp.stack([reduce_rows(token_all, cat[1 + s]) for s in range(3)])
    return (input_grad, qkv_grad, proj_grad)


def solution(mesh):
    placed = (
        P("dp", "ctx", "space", None),
        P("dp", "ctx", "space", None),
        P(None, None, "space"),
        P(None, "space"),
    )
    sizes = tuple(mesh.shape[a] for a in ("dp", "ctx", "space"))
    return jax.shard_map(
        functools.partial(body, sizes),
        mesh=mesh,
        in_specs=placed,
        out_specs=(
            P("dp", "ctx", "space", None),
            P(None, ("dp", "ctx"), "space"),
            P(("dp", "ctx"), "space"),
        ),
        check_vma=False,
    )
```

```python
import functools
import math

import jax
import jax.numpy as jnp
from jax import lax
from jax.experimental import pallas as pl
from jax.experimental.pallas import tpu as pltpu
from jax.sharding import PartitionSpec as P

HS = 128
F32 = jnp.float32
BF16 = jnp.bfloat16
SCALE = 1.0 / math.sqrt(HS)


FREE = pl.CostEstimate(flops=1, bytes_accessed=1, transcendentals=0)
PARAMS = pltpu.CompilerParams(vmem_limit_bytes=60 * 1024 * 1024)
SMALL = pltpu.CompilerParams(vmem_limit_bytes=40 * 1024 * 1024)


def softmax_row(q, keys):
    scores = [jnp.sum(q * k, axis=-1, keepdims=True) * SCALE for k in keys]
    top = functools.reduce(jnp.maximum, scores)
    expo = [jnp.exp(s - top) for s in scores]
    total = functools.reduce(jnp.add, expo)
    return [e / total for e in expo]


def weighted(weights, values):
    return functools.reduce(jnp.add, [w * v for w, v in zip(weights, values)])


def rounded(values):
    return [v.astype(BF16).astype(F32) for v in values]


def forward_kernel(frames, heads, slot_ref, q_ref, k_ref, v_ref, att_ref):
    slots = [slot_ref[f] for f in range(frames)]
    for h in range(heads):
        cols = pl.ds(h * HS, HS)
        q, k, v = (
            [ref[0, slots[f], :, cols].astype(F32) for f in range(frames)]
            for ref in (q_ref, k_ref, v_ref)
        )
        for f in range(frames):
            probs_b = rounded(softmax_row(q[f], k[: f + 1]))
            att_ref[0, slots[f], :, cols] = weighted(probs_b, v).astype(BF16)


def backward_kernel(frames, heads, slot_ref, q_ref, k_ref, v_ref, near_ref, far_ref, dq_ref, dk_ref, dv_ref):
    slots = [slot_ref[f] for f in range(frames)]
    for h in range(heads):
        cols = pl.ds(h * HS, HS)
        q, k, v = (
            [ref[0, slots[f], :, cols].astype(F32) for f in range(frames)]
            for ref in (q_ref, k_ref, v_ref)
        )
        far = far_ref[0, 0, :, cols].astype(F32)
        o = [
            jnp.where(
                slots[f] == frames - 1,
                far,
                near_ref[0, jnp.minimum(slots[f], frames - 2), :, cols].astype(F32),
            )
            for f in range(frames)
        ]
        dk = [None] * frames
        dv = [None] * frames
        for f in range(frames):
            probs = softmax_row(q[f], k[: f + 1])
            probs_b = rounded(probs)
            dprobs = [jnp.sum(o[f] * v[g], axis=-1, keepdims=True) for g in range(f + 1)]
            inner = weighted(probs, dprobs)
            dscores = rounded([p * (d - inner) for p, d in zip(probs, dprobs)])
            dq = weighted(dscores, k)
            dq_ref[0, slots[f], :, cols] = (dq * SCALE).astype(BF16)
            for g in range(f + 1):
                add_k, add_v = dscores[g] * q[f], probs_b[g] * o[f]
                dk[g] = add_k if dk[g] is None else dk[g] + add_k
                dv[g] = add_v if dv[g] is None else dv[g] + add_v
        for g in range(frames):
            dk_ref[0, slots[g], :, cols] = (dk[g] * SCALE).astype(BF16)
            dv_ref[0, slots[g], :, cols] = dv[g].astype(BF16)


def per_group(kernel, slots, args, count):
    groups, frames, patches, width = args[0].shape

    def block(shape):
        return pl.BlockSpec((1,) + shape[1:], lambda i, slot_ref: (i, 0, 0, 0))

    out = jax.ShapeDtypeStruct(args[0].shape, BF16)
    return pl.pallas_call(
        functools.partial(kernel, frames, width // HS),
        grid_spec=pltpu.PrefetchScalarGridSpec(
            num_scalar_prefetch=1,
            grid=(groups,),
            in_specs=[block(a.shape) for a in args],
            out_specs=[block(out.shape)] * count,
        ),
        out_shape=[out] * count,
        compiler_params=SMALL,
        cost_estimate=FREE,
    )(slots, *args)


def mxu(a, b, contract):
    return lax.dot_general(a, b, ((contract[:1], contract[1:]), ((), ())), preferred_element_type=F32)


def block_of(extent, most):
    size = most - most % 128
    while extent % size:
        size -= 128
    return size


def in_order(sets):
    pieces = []
    for e in range(2 * len(sets[0])):
        for held in sets:
            array = held[e // 2]
            size = array.shape[1] * array.shape[2]
            pieces.append((array.reshape(-1, array.shape[-1]), size, e % 2))
    return pieces


def project(sets, weights):
    pieces = in_order(sets)
    count, model, width = weights.shape
    total = sum(size for _, size, _ in pieces)

    def kernel(*refs):
        x_refs, w_ref, x_ref = refs[: len(pieces)], refs[len(pieces)], refs[-1]
        step = pl.program_id(0)

        @pl.when(step == 0)
        def _():
            row = 0
            for ref, (_, size, _) in zip(x_refs, pieces):
                x_ref[row : row + size] = ref[...]
                row += size

        product = mxu(x_ref[...], w_ref[0], (1, 0)).astype(BF16)
        for s, out_ref in enumerate(refs[len(pieces) + 1 : -1]):

            @pl.when(step == s)
            def _():
                out_ref[...] = product

    out = jax.ShapeDtypeStruct((total, width), BF16)
    outs = pl.pallas_call(
        kernel,
        grid=(count,),
        in_specs=[pl.BlockSpec((size, model), lambda i, at=at: (at, 0)) for _, size, at in pieces]
        + [pl.BlockSpec((1, model, width), lambda i: (i, 0, 0))],
        out_specs=[pl.BlockSpec(out.shape, lambda i: (0, 0))] * count,
        out_shape=[out] * count,
        scratch_shapes=[pltpu.VMEM((total, model), BF16)],
        compiler_params=SMALL,
        cost_estimate=FREE,
    )(*[array for array, _, _ in pieces], weights)
    rows = sets[0][0].shape[2]
    return [o.reshape(2 * len(sets[0]), -1, rows, width) for o in outs]


def outer(sets, grads, column, share, dtype, plus=None):
    pieces = in_order(sets)
    width = grads[0].shape[-1]
    count = len(grads)
    wide = block_of(share, 768)
    steps = share // wide
    extra = [] if plus is None else [plus]

    def kernel(column_ref, *refs):
        x = jnp.concatenate([ref[...] for ref in refs[: len(pieces)]], 0)
        grad_refs = refs[len(pieces) : len(pieces) + count]
        for grad_ref, out_ref in zip(grad_refs, refs[-count:]):
            total = mxu(x, grad_ref[...], (0, 0))
            if extra:
                total = total + refs[len(pieces) + count][...]
            out_ref[...] = total.astype(dtype)

    grads = [g.reshape(-1, width) for g in grads]
    out = jax.ShapeDtypeStruct((share, width), dtype)
    tile = pl.BlockSpec((wide, width), lambda i, c: (i, 0))
    return pl.pallas_call(
        kernel,
        grid_spec=pltpu.PrefetchScalarGridSpec(
            num_scalar_prefetch=1,
            grid=(steps,),
            in_specs=[
                pl.BlockSpec((size, wide), lambda i, c, at=at: (at, c[0] * steps + i))
                for _, size, at in pieces
            ]
            + [pl.BlockSpec(g.shape, lambda i, c: (0, 0)) for g in grads]
            + [tile] * len(extra),
            out_specs=[tile] * count,
        ),
        out_shape=[out] * count,
        compiler_params=PARAMS,
        cost_estimate=FREE,
    )(jnp.asarray(column, jnp.int32).reshape(1), *[array for array, _, _ in pieces], *grads, *extra)


def backproject(grads, block, rows, weights, splits=None):
    _, model, width = weights[0].shape
    wide = block_of(model, 512)
    splits = splits or [rows]
    count = len(grads)

    def kernel(*refs):
        w_refs, out_refs = refs[count : count + len(weights)], refs[-len(splits) :]
        matrices = [w_ref[s] for w_ref in w_refs for s in range(w_ref.shape[0])]
        total = sum(mxu(ref[...], w, (1, 1)) for ref, w in zip(refs[:count], matrices))
        row = 0
        for size, out_ref in zip(splits, out_refs):
            out_ref[...] = total[row : row + size].astype(BF16)
            row += size

    return pl.pallas_call(
        kernel,
        grid=(model // wide,),
        in_specs=[pl.BlockSpec((rows, width), lambda i: (block, 0))] * count
        + [pl.BlockSpec((w.shape[0], wide, width), lambda i: (0, i, 0)) for w in weights],
        out_specs=[pl.BlockSpec((size, wide), lambda i: (0, i)) for size in splits],
        out_shape=[jax.ShapeDtypeStruct((size, model), BF16) for size in splits],
        compiler_params=PARAMS,
        cost_estimate=FREE,
    )(*[g.reshape(-1, width) for g in grads], *weights)


def placed_at(pieces, where):
    shape = pieces[0].shape
    count = len(pieces)

    def kernel(where_ref, *refs):
        for i in range(count):

            @pl.when(pl.program_id(0) == i)
            def _():
                refs[-1][0] = refs[i][...]

    return pl.pallas_call(
        kernel,
        grid_spec=pltpu.PrefetchScalarGridSpec(
            num_scalar_prefetch=1,
            grid=(count,),
            in_specs=[pl.BlockSpec(shape, lambda i, w: (0, 0))] * count,
            out_specs=pl.BlockSpec((1,) + shape, lambda i, w: (w[i], 0, 0)),
        ),
        out_shape=jax.ShapeDtypeStruct((count,) + shape, pieces[0].dtype),
        compiler_params=PARAMS,
        cost_estimate=FREE,
    )(where, *pieces)


def tie(x, *first):
    return lax.optimization_barrier((x, *first))[0]


def tie_all(*x):
    return lax.optimization_barrier(x)


def body(sizes, inputs, upstream, qkv_weight, out_weight):
    n_dp, n, n_space = sizes
    me = lax.axis_index("ctx")
    me_dp = lax.axis_index("dp")
    clips, single, patches, model = inputs.shape
    width = qkv_weight.shape[2]
    rows = clips * single * patches // n
    bits = [1 << i for i in range(n_space.bit_length() - 1)][::-1]
    order = [0] + [d for d in range(1, n) if d != n // 2] + [n // 2]
    place = {d: i for i, d in enumerate(order)}
    slots = jnp.array([place[d] for d in range(n)], jnp.int32)[
        lax.rem(me - jnp.arange(n) + n, n)
    ]
    home, others, across = order[:1], order[1:-1], order[-1:]

    def shift(x, d):
        return lax.ppermute(x, "ctx", [(i, (i + d) % n) for i in range(n)])

    def flip(x, bit):
        return lax.ppermute(x, "space", [(i, i ^ bit) for i in range(n_space)])

    def swap(x):
        return lax.ppermute(x, "dp", [(0, 1), (1, 0)])

    def to(x, d):
        x = x.reshape(n, rows, model)
        return lax.dynamic_index_in_dim(x, lax.rem(me + d, n), 0, keepdims=False)

    def spread(held):
        held = [held]
        for bit in bits[1:]:
            held = held + [flip(h, bit) for h in held]
        return held

    share = model // n_dp

    def lend(held):
        return swap(lax.dynamic_slice_in_dim(held, (1 - me_dp) * share, share, 3))

    def cut(x, ds):
        return [to(x, d) for d in ds]

    def moved(pieces, ds):
        return [shift(p, d) for p, d in zip(pieces, ds)]

    here_hi, here_hu = to(inputs, 0)[None], to(upstream, 0)[None]
    send_ci, send_cu, send_bu = cut(inputs, others), cut(upstream, others), cut(upstream, across)

    near_bi = moved(cut(inputs, across), across)
    there_hi, there_hu = flip(here_hi, bits[0]), flip(here_hu, bits[0])
    weights = [qkv_weight, flip(qkv_weight, bits[-1])]
    near_bi, there_hi, there_hu, weights, send_ci, send_cu, send_bu = tie_all(
        near_bi, there_hi, there_hu, weights, send_ci, send_cu, send_bu
    )

    pair_hi, pair_hu = jnp.stack([here_hi, there_hi]), jnp.stack([here_hu, there_hu])
    here_bi = jnp.stack(near_bi)
    near_ci = moved(send_ci, others)
    there_bi = flip(here_bi, bits[0])
    lent_hi = lend(pair_hi)
    all_hi = spread(pair_hi)
    near_ci, there_bi, lent_hi, all_hi, pair_hu, send_cu, send_bu = tie_all(
        near_ci, there_bi, lent_hi, all_hi, pair_hu, send_cu, send_bu
    )

    pair_bi = jnp.stack([here_bi, there_bi])
    here_ci = jnp.stack(near_ci)
    near_cu = moved(send_cu, others)
    there_ci = flip(here_ci, bits[0])
    lent_bi = lend(pair_bi)
    all_bi = spread(pair_bi)
    near_cu, there_ci, lent_bi, all_bi, pair_hu, lent_hi, send_bu = tie_all(
        near_cu, there_ci, lent_bi, all_bi, pair_hu, lent_hi, send_bu
    )

    pair_ci = jnp.stack([here_ci, there_ci])
    here_cu = jnp.stack(near_cu)
    near_bu = moved(send_bu, across)
    there_cu = flip(here_cu, bits[0])
    lent_ci = lend(pair_ci)
    all_ci = spread(pair_ci)
    tokens = [all_hi, all_ci, all_bi]
    q, k, v = project(tokens, qkv_weight)
    near_bu, there_cu, lent_ci, q, k, v, lent_hi, lent_bi, pair_hu = tie_all(
        near_bu, there_cu, lent_ci, q, k, v, lent_hi, lent_bi, pair_hu
    )

    pair_cu = jnp.stack([here_cu, there_cu])
    here_bu = jnp.stack(near_bu)
    there_bu = flip(here_bu, bits[0])
    all_hu, all_cu = spread(pair_hu), spread(pair_cu)
    from_hi, from_bi = spread(lent_hi), spread(lent_bi)
    (o_near,) = project([all_hu, all_cu], out_weight[None])
    there_bu, from_hi, from_bi, o_near, all_hu, all_cu, lent_ci = tie_all(
        there_bu, from_hi, from_bi, o_near, all_hu, all_cu, lent_ci
    )

    all_bu = spread(jnp.stack([here_bu, there_bu]))
    (o_far,) = project([all_bu], out_weight[None])
    ups = [all_hu, all_cu, all_bu]
    grads = list(per_group(backward_kernel, slots, (q, k, v, o_near, o_far), 3))
    grads = list(tie_all(*grads))

    def along_ctx(term):
        return lax.psum_scatter(term, "ctx", scatter_dimension=0, tiled=True)

    def summed(a, b):
        return (a.astype(F32) + b.astype(F32)).astype(BF16)

    for _ in bits[2:]:
        raise NotImplementedError
    crossed = swap(grads[0])
    got = flip(jnp.stack([g[n_space // 2 :] for g in grads]), bits[-1])
    lent = [from_hi, spread(lent_ci), from_bi]
    mine = outer(tokens, grads, me_dp, share, F32)
    (att,) = per_group(forward_kernel, slots, (q, k, tie(v, mine[0])), 1)
    (proj_send,) = outer(ups, [att], 1 - me_dp, share, BF16)
    crossed, got, lent, mine, att, proj_send, grads = tie_all(
        crossed, got, lent, mine, att, proj_send, grads
    )

    moving = swap(grads[1])
    (term,) = outer(lent, [crossed], 0, share, BF16, mine[0])
    sums = [along_ctx(term)]
    parts = [tie(g, term) for g in grads] + [got[s] for s in range(3)]
    home, mid, far = backproject(parts, 1, n * rows, weights, [rows, (n - 2) * rows, rows])
    crossed, home, mid, far, mine, grads, parts = tie_all(
        moving, home, mid, far, mine, grads, parts
    )

    moving = swap(grads[2])
    far_there, mid_there = flip(far, bits[0]), flip(mid, bits[0])
    (term,) = outer(lent, [crossed], 0, share, BF16, mine[1])
    kept = backproject([tie(p, term) for p in parts], 0, n * rows, weights, [rows] * n)
    sums.append(along_ctx(tie(term, sums[-1])))
    crossed, far_there, mid_there, mine, kept, proj_send, sums[0] = tie_all(
        moving, far_there, mid_there, mine, kept, proj_send, sums[0]
    )

    moving = swap(proj_send)
    home_there = flip(home, bits[0])
    back = {across[0]: shift(summed(kept[n - 1], far_there), n - across[0])}
    mid_sums = [
        summed(kept[1 + i], mid_there[i * rows : (i + 1) * rows]) for i in range(n - 2)
    ]
    (term,) = outer(lent, [crossed], 0, share, BF16, mine[2])
    (proj_mine,) = outer(ups, [tie(att, term)], me_dp, share, F32)
    sums.append(along_ctx(tie(term, sums[-1])))
    crossed, home_there, back, mid_sums, proj_mine, sums[1] = tie_all(
        moving, home_there, back, mid_sums, proj_mine, sums[1]
    )

    for i, d in enumerate(others):
        back[d] = shift(mid_sums[i], n - d)
    back[0] = summed(kept[0], home_there)
    term = summed(proj_mine, crossed)
    where = lax.rem(jnp.arange(n, dtype=jnp.int32) + me, n)
    input_grad = placed_at([back[d] for d in range(n)], where)
    sums.append(along_ctx(tie(term, sums[-1], input_grad)))
    qkv_grad = jnp.stack([x.astype(F32) for x in sums[:3]])
    return (input_grad.reshape(inputs.shape), qkv_grad, sums[3].astype(F32))


def solution(mesh):
    placed = (
        P("dp", "ctx", "space", None),
        P("dp", "ctx", "space", None),
        P(None, None, "space"),
        P(None, "space"),
    )
    sizes = tuple(mesh.shape[a] for a in ("dp", "ctx", "space"))
    return jax.shard_map(
        functools.partial(body, sizes),
        mesh=mesh,
        in_specs=placed,
        out_specs=(
            P("dp", "ctx", "space", None),
            P(None, ("dp", "ctx"), "space"),
            P(("dp", "ctx"), "space"),
        ),
        check_vma=False,
    )
```

```python
import functools
import math

import jax
import jax.numpy as jnp
from jax import lax
from jax.experimental import pallas as pl
from jax.experimental.pallas import tpu as pltpu
from jax.sharding import PartitionSpec as P

HS = 128
F32 = jnp.float32
BF16 = jnp.bfloat16
SCALE = 1.0 / math.sqrt(HS)


FREE = pl.CostEstimate(flops=1, bytes_accessed=1, transcendentals=0)
MIB = 1024 * 1024


def softmax_row(q, keys):
    scores = [jnp.sum(q * k, axis=-1, keepdims=True) * SCALE for k in keys]
    top = functools.reduce(jnp.maximum, scores)
    expo = [jnp.exp(s - top) for s in scores]
    total = functools.reduce(jnp.add, expo)
    return [e / total for e in expo]


def weighted(weights, values):
    return functools.reduce(jnp.add, [w * v for w, v in zip(weights, values)])


def rounded(values):
    return [v.astype(BF16).astype(F32) for v in values]


def forward_kernel(frames, heads, slot_ref, q_ref, k_ref, v_ref, att_ref):
    slots = [slot_ref[f] for f in range(frames)]
    for h in range(heads):
        cols = pl.ds(h * HS, HS)
        q, k, v = (
            [ref[0, slots[f], :, cols].astype(F32) for f in range(frames)]
            for ref in (q_ref, k_ref, v_ref)
        )
        for f in range(frames):
            probs_b = rounded(softmax_row(q[f], k[: f + 1]))
            att_ref[0, slots[f], :, cols] = weighted(probs_b, v).astype(BF16)


def backward_kernel(frames, heads, slot_ref, q_ref, k_ref, v_ref, near_ref, far_ref, dq_ref, dk_ref, dv_ref, give_ref):
    slots = [slot_ref[f] for f in range(frames)]
    for h in range(heads):
        cols = pl.ds(h * HS, HS)
        q, k, v = (
            [ref[0, slots[f], :, cols].astype(F32) for f in range(frames)]
            for ref in (q_ref, k_ref, v_ref)
        )
        far = far_ref[0, 0, :, cols].astype(F32)
        o = [
            jnp.where(
                slots[f] == frames - 1,
                far,
                near_ref[0, jnp.minimum(slots[f], frames - 2), :, cols].astype(F32),
            )
            for f in range(frames)
        ]
        dk = [None] * frames
        dv = [None] * frames
        for f in range(frames):
            probs = softmax_row(q[f], k[: f + 1])
            probs_b = rounded(probs)
            dprobs = [jnp.sum(o[f] * v[g], axis=-1, keepdims=True) for g in range(f + 1)]
            inner = weighted(probs, dprobs)
            dscores = rounded([p * (d - inner) for p, d in zip(probs, dprobs)])
            dq = weighted(dscores, k)
            dq_ref[0, slots[f], :, cols] = give_ref[0, 0, slots[f], :, cols] = (dq * SCALE).astype(BF16)
            for g in range(f + 1):
                add_k, add_v = dscores[g] * q[f], probs_b[g] * o[f]
                dk[g] = add_k if dk[g] is None else dk[g] + add_k
                dv[g] = add_v if dv[g] is None else dv[g] + add_v
        for g in range(frames):
            dk_ref[0, slots[g], :, cols] = give_ref[1, 0, slots[g], :, cols] = (dk[g] * SCALE).astype(BF16)
            dv_ref[0, slots[g], :, cols] = give_ref[2, 0, slots[g], :, cols] = dv[g].astype(BF16)


def per_group(kernel, slots, args, backward):
    groups, frames, patches, width = args[0].shape
    def block(shape):
        return pl.BlockSpec((1,) + shape[1:], lambda i, slot_ref: (i, 0, 0, 0))

    out = jax.ShapeDtypeStruct(args[0].shape, BF16)
    count = 3 if backward else 1
    outs, specs = [out] * count, [block(out.shape)] * count
    if backward:
        half = groups // 2
        outs.append(jax.ShapeDtypeStruct((3, half) + out.shape[1:], BF16))
        specs.append(
            pl.BlockSpec(
                (3, 1) + out.shape[1:], lambda i, slot_ref: (0, jnp.maximum(i - half, 0), 0, 0, 0)
            )
        )
    return pl.pallas_call(
        functools.partial(kernel, frames, width // HS),
        grid_spec=pltpu.PrefetchScalarGridSpec(
            num_scalar_prefetch=1,
            grid=(groups,),
            in_specs=[block(a.shape) for a in args],
            out_specs=specs,
        ),
        out_shape=outs,
        compiler_params=pltpu.CompilerParams(vmem_limit_bytes=12 * MIB),
        cost_estimate=FREE,
    )(slots, *args)


def mxu(a, b, contract):
    return lax.dot_general(a, b, ((contract[:1], contract[1:]), ((), ())), preferred_element_type=F32)


def block_of(extent, most):
    size = most - most % 128
    while extent % size:
        size -= 128
    return size


def in_order(sets):
    pieces = []
    for e in range(len(sets[0])):
        for held in sets:
            array, block = held[e]
            size = array.shape[1] * array.shape[2]
            pieces.append((array.reshape(-1, array.shape[-1]), size, block))
    return pieces


def project(sets, weights, grant=28):
    pieces = in_order(sets)
    count, model, width = weights.shape
    total = sum(size for _, size, _ in pieces)

    def kernel(*refs):
        x_refs, w_ref, x_ref = refs[: len(pieces)], refs[len(pieces)], refs[-1]
        step = pl.program_id(0)

        @pl.when(step == 0)
        def _():
            row = 0
            for ref, (_, size, _) in zip(x_refs, pieces):
                x_ref[row : row + size] = ref[...]
                row += size

        product = mxu(x_ref[...], w_ref[0], (1, 0)).astype(BF16)
        for s, out_ref in enumerate(refs[len(pieces) + 1 : -1]):

            @pl.when(step == s)
            def _():
                out_ref[...] = product

    out = jax.ShapeDtypeStruct((total, width), BF16)
    outs = pl.pallas_call(
        kernel,
        grid=(count,),
        in_specs=[
            pl.BlockSpec((size, model), lambda i, at=at: (at, 0), pipeline_mode=pl.Buffered(1))
            for _, size, at in pieces
        ]
        + [pl.BlockSpec((1, model, width), lambda i: (i, 0, 0))],
        out_specs=[pl.BlockSpec(out.shape, lambda i: (0, 0))] * count,
        out_shape=[out] * count,
        scratch_shapes=[pltpu.VMEM((total, model), BF16)],
        compiler_params=pltpu.CompilerParams(vmem_limit_bytes=grant * MIB),
        cost_estimate=FREE,
    )(*[array for array, _, _ in pieces], weights)
    rows = sets[0][0][0].shape[2]
    return [o.reshape(len(sets[0]), -1, rows, width) for o in outs]


def outer(sets, grads, column, share, dtype, plus=None, window=None, also=None):
    pieces = in_order(sets)
    more = in_order(also[0]) if also else []
    width = grads[0][0].shape[-1]
    count = len(grads)
    tall = sum(size for _, size, _ in pieces)
    wide = block_of(share, 768)
    steps = share // wide
    extra = [] if plus is None else [plus]
    shards, start = window or (1, 0)
    high = share // shards
    inside = wide // high

    def kernel(scalars_ref, *refs):
        x = jnp.concatenate([ref[...] for ref in refs[: len(pieces)]], 0)
        refs = refs[len(pieces) :]
        if also:
            x_more = jnp.concatenate([ref[...] for ref in refs[: len(more)]], 0)
            more_ref, refs = refs[len(more)], refs[len(more) + 1 :]
        grad_refs, out_refs = refs[:count], refs[count + len(extra) :]
        for grad_ref, out_ref in zip(grad_refs, out_refs):
            total = mxu(x, grad_ref[...], (0, 0))
            if also:
                total = total + mxu(x_more, more_ref[...], (0, 0))
            if extra:
                total = total + refs[count][...]
            total = total.astype(dtype)
            out_ref[...] = total
            if window:
                for j in range(inside):
                    at = pl.program_id(0) * inside + j - scalars_ref[1]

                    @pl.when((at >= 0) & (at < shards - 1))
                    def _():
                        out_refs[1][at] = total[j * high : (j + 1) * high]

    out = jax.ShapeDtypeStruct((share, width), dtype)
    tile = pl.BlockSpec((wide, width), lambda i, c: (i, 0))
    outs, specs = [out] * count, [tile] * count
    if window:
        outs.append(jax.ShapeDtypeStruct((shards - 1, high, width), dtype))
        specs.append(pl.BlockSpec(outs[-1].shape, lambda i, c: (0, 0, 0)))
    return pl.pallas_call(
        kernel,
        grid_spec=pltpu.PrefetchScalarGridSpec(
            num_scalar_prefetch=1,
            grid=(steps,),
            in_specs=[
                pl.BlockSpec((size, wide), lambda i, c, at=at: (at, c[0] * steps + i))
                for _, size, at in pieces
            ]
            + [
                pl.BlockSpec((size, wide), lambda i, c, at=at: (at, c[2] * steps + i))
                for _, size, at in more
            ]
            + [pl.BlockSpec((tall, width), lambda i, c: (also[1][1], 0))] * bool(also)
            + [pl.BlockSpec((tall, width), lambda i, c, at=at: (at, 0)) for _, at in grads]
            + [tile] * len(extra),
            out_specs=specs,
        ),
        out_shape=outs,
        compiler_params=pltpu.CompilerParams(vmem_limit_bytes=58 * MIB),
        cost_estimate=FREE,
    )(
        jnp.stack([jnp.asarray(x, jnp.int32) for x in (column, start, also[2] if also else 0)]),
        *[array for array, _, _ in pieces],
        *[array for array, _, _ in more],
        *([also[1][0].reshape(-1, width)] if also else []),
        *[g.reshape(-1, width) for g, _ in grads],
        *extra,
    )


def backproject(grads, more, block, rows, weights, splits):
    count, model, width = weights[0].shape
    wide = block_of(model, 512)
    halves = more.size // (count * width * rows) * 2

    def kernel(*refs):
        more_ref, w_refs, out_refs = refs[count], refs[count + 1 : count + 3], refs[count + 3 :]
        total = sum(
            mxu(refs[s][...], w_refs[0][s], (1, 1)) + mxu(more_ref[s], w_refs[1][s], (1, 1))
            for s in range(count)
        )
        row = 0
        for size, out_ref in zip(splits, out_refs):
            out_ref[...] = total[row : row + size].astype(BF16)
            row += size

    return pl.pallas_call(
        kernel,
        grid=(model // wide,),
        in_specs=[pl.BlockSpec((rows, width), lambda i, at=at: (halves * at + block, 0)) for _, at in grads]
        + [pl.BlockSpec((count, rows, width), lambda i: (0, block, 0))]
        + [pl.BlockSpec((count, wide, width), lambda i: (0, i, 0))] * 2,
        out_specs=[pl.BlockSpec((size, wide), lambda i: (0, i)) for size in splits],
        out_shape=[jax.ShapeDtypeStruct((size, model), BF16) for size in splits],
        compiler_params=pltpu.CompilerParams(vmem_limit_bytes=58 * MIB),
        cost_estimate=FREE,
    )(*[g.reshape(-1, width) for g, _ in grads], more.reshape(count, -1, width), *weights)


def placed_at(pieces, where):
    shape = pieces[0].shape
    count = len(pieces)

    def kernel(where_ref, *refs):
        for i in range(count):

            @pl.when(pl.program_id(0) == i)
            def _():
                refs[-1][0] = refs[i][...]

    return pl.pallas_call(
        kernel,
        grid_spec=pltpu.PrefetchScalarGridSpec(
            num_scalar_prefetch=1,
            grid=(count,),
            in_specs=[pl.BlockSpec(shape, lambda i, w: (0, 0))] * count,
            out_specs=pl.BlockSpec((1,) + shape, lambda i, w: (w[i], 0, 0)),
        ),
        out_shape=jax.ShapeDtypeStruct((count,) + shape, pieces[0].dtype),
        compiler_params=pltpu.CompilerParams(vmem_limit_bytes=6 * MIB),
        cost_estimate=FREE,
    )(where, *pieces)


def finished(chains, at):
    arrays = [x for chain in chains for x in chain]
    _, rows, width = arrays[0].shape

    def kernel(at_ref, *refs):
        i = 0
        for c, chain in enumerate(chains):
            refs[-1][c] = sum(ref[0].astype(F32) for ref in refs[i : i + len(chain)])
            i += len(chain)

    return pl.pallas_call(
        kernel,
        grid_spec=pltpu.PrefetchScalarGridSpec(
            num_scalar_prefetch=1,
            grid=(1,),
            in_specs=[
                pl.BlockSpec((1, rows, width), lambda i, at_ref, j=j: (at_ref[j], 0, 0))
                for j in range(len(arrays))
            ],
            out_specs=pl.BlockSpec((len(chains), rows, width), lambda i, at_ref: (0, 0, 0)),
        ),
        out_shape=jax.ShapeDtypeStruct((len(chains), rows, width), F32),
        compiler_params=pltpu.CompilerParams(vmem_limit_bytes=60 * MIB),
        cost_estimate=FREE,
    )(jnp.stack(at).astype(jnp.int32), *arrays)


def tie(x, *first):
    return lax.optimization_barrier((x, *first))[0]


def paced(x):
    mark = pl.pallas_call(
        lambda x_ref, out_ref: out_ref.__setitem__(..., jnp.zeros_like(out_ref)),
        in_specs=[pl.BlockSpec(memory_space=pl.ANY)],
        out_shape=jax.ShapeDtypeStruct((8, 128), F32),
        cost_estimate=pl.CostEstimate(flops=20 * 10**9, bytes_accessed=1, transcendentals=0),
    )(x)
    return tie(x, mark)


def tie_all(*x):
    leaves, tree = jax.tree.flatten(x)
    arrays = iter(lax.optimization_barrier([y for y in leaves if not isinstance(y, int)]))
    return jax.tree.unflatten(tree, [y if isinstance(y, int) else next(arrays) for y in leaves])


def body(sizes, inputs, upstream, qkv_weight, out_weight):
    n_dp, n, n_space = sizes
    me = lax.axis_index("ctx")
    me_dp = lax.axis_index("dp")
    clips, single, patches, model = inputs.shape
    width = qkv_weight.shape[2]
    rows = clips * single * patches // n
    bits = [1 << i for i in range(n_space.bit_length() - 1)][::-1]
    order = [0] + [d for d in range(1, n) if d != n // 2] + [n // 2]
    place = {d: i for i, d in enumerate(order)}
    slots = jnp.array([place[d] for d in range(n)], jnp.int32)[
        lax.rem(me - jnp.arange(n) + n, n)
    ]
    home, others, across = order[:1], order[1:-1], order[-1:]

    def shift(x, d):
        return lax.ppermute(x, "ctx", [(i, (i + d) % n) for i in range(n)])

    def flip(x, bit):
        return lax.ppermute(x, "space", [(i, i ^ bit) for i in range(n_space)])

    def swap(x):
        return lax.ppermute(x, "dp", [(0, 1), (1, 0)])

    def to(x, d):
        x = x.reshape(n, rows, model)
        return lax.dynamic_index_in_dim(x, lax.rem(me + d, n), 0, keepdims=False)

    def spread(*held):
        held = list(held)
        for bit in bits[1:]:
            held = held + [flip(h, bit) for h in held]
        return [(h, block) for h in held for block in range(h.shape[0])]

    share = model // n_dp

    def lend(held):
        return swap(lax.dynamic_slice_in_dim(held, (1 - me_dp) * share, share, 3))

    def cut(x, ds):
        return [to(x, d) for d in ds]

    def moved(pieces, ds):
        return [shift(p, d) for p, d in zip(pieces, ds)]

    here_hi, here_hu = to(inputs, 0)[None], to(upstream, 0)[None]
    send_ci, send_cu, send_bu = cut(inputs, others), cut(upstream, others), cut(upstream, across)

    near_bi = moved(cut(inputs, across), across)
    there_hi, there_hu = flip(here_hi, bits[0]), flip(here_hu, bits[0])
    weights = [qkv_weight, flip(qkv_weight, bits[-1])]
    near_bi, there_hi, there_hu, weights, send_ci, send_cu, send_bu = tie_all(
        near_bi, there_hi, there_hu, weights, send_ci, send_cu, send_bu
    )

    pair_hi, pair_hu = jnp.stack([here_hi, there_hi]), jnp.stack([here_hu, there_hu])
    here_bi = jnp.stack(near_bi)
    near_ci = moved(send_ci, others)
    there_bi = flip(here_bi, bits[0])
    lent_hi = lend(pair_hi)
    all_hi = spread(pair_hi)
    near_ci, there_bi, lent_hi, all_hi, pair_hu, send_cu, send_bu = tie_all(
        near_ci, there_bi, lent_hi, all_hi, pair_hu, send_cu, send_bu
    )

    pair_bi = jnp.stack([here_bi, there_bi])
    here_ci = jnp.stack(near_ci)
    near_cu = moved(send_cu, others)
    there_ci = flip(here_ci, bits[0])
    lent_bi = lend(pair_bi)
    all_bi = spread(pair_bi)
    near_cu, there_ci, lent_bi, all_bi, pair_hu, lent_hi, send_bu = tie_all(
        near_cu, there_ci, lent_bi, all_bi, pair_hu, lent_hi, send_bu
    )

    pair_ci = jnp.stack([here_ci, there_ci])
    here_cu = jnp.stack(near_cu)
    near_bu = moved(send_bu, across)
    there_cu = flip(here_cu, bits[0])
    lent_ci = lend(pair_ci)
    all_ci = spread(pair_ci)
    tokens = [all_hi, all_ci, all_bi]
    q, k, v = project(tokens, qkv_weight)
    near_bu, there_cu, lent_ci, q, k, v, lent_hi, lent_bi, pair_hu = tie_all(
        near_bu, there_cu, lent_ci, q, k, v, lent_hi, lent_bi, pair_hu
    )

    pair_cu = jnp.stack([here_cu, there_cu])
    here_bu = jnp.stack(near_bu)
    there_bu = flip(here_bu, bits[0])
    all_hu, all_cu = spread(pair_hu), spread(pair_cu)
    here_bu = spread(here_bu[None])
    from_hi = spread(lent_hi)
    (o_near,) = project([all_hu, all_cu], out_weight[None])
    there_bu, from_hi, here_bu, o_near, all_hu, all_cu, lent_ci, lent_bi = tie_all(
        there_bu, from_hi, here_bu, o_near, all_hu, all_cu, lent_ci, lent_bi
    )

    there_bu = spread(there_bu[None])
    all_bu = [x for pair in zip(here_bu, there_bu) for x in pair]
    (o_far,) = project([all_bu], out_weight[None], 58)
    ups = [all_hu, all_cu, all_bu]
    *grads, give = per_group(backward_kernel, slots, (q, k, v, o_near, o_far), True)
    grads, give, lent_ci, lent_bi = tie_all(grads, give, lent_ci, lent_bi)

    chains, arrived, first = [], [], []

    def total(arrays):
        return sum(x.astype(F32) for x in arrays)

    def to_send(c, step):
        count = n - 1 - step
        start = jnp.where(me == step, step + 1, 0)
        terms = [lax.dynamic_slice_in_dim(t, start, count, 0) for t in chains[c]]
        if step:
            at = jnp.where(me == step, 1, 0)
            terms.append(lax.dynamic_slice_in_dim(arrived[c][-1], at, count, 0))
        return total(terms).astype(BF16)

    def begin(terms, send=None):
        chains.append([t.reshape(n, share // n, width) for t in terms])
        arrived.append([])
        first.append(to_send(len(chains) - 1, 0) if send is None else send)

    def crossed_term(came, plus, also=None):
        window = (n, jnp.where(me == 0, 1, 0))
        term, send = outer(lent, [(came, 0)], 0, share, BF16, plus, window, also)
        begin([term], send)
        return term

    def advance(c):
        step = len(arrived[c])
        if step == n - 1:
            return
        send = to_send(c, step) if step else first[c]
        came = lax.ppermute(send, "ctx", [(step, step + 1), (n - 1 - step, n - 2 - step)])
        arrived[c].append(came if step else paced(came))

    def ended(cs):
        all_arrays, at = [], []
        for c in cs:
            all_arrays.append(chains[c] + arrived[c])
            at += [me] * len(chains[c])
            for step in range(n - 1):
                at.append(jnp.where(me == step + 1, 0, n - 2 - step))
        return finished(all_arrays, at)

    for _ in bits[2:]:
        raise NotImplementedError
    crossed = swap(grads[0])
    got = flip(give, bits[-1])
    lent = [from_hi, spread(lent_ci), spread(lent_bi)]
    grads = [(g, 0) for g in grads]
    splits = [rows] * (n + 1) + [(n - 2) * rows, rows]
    *kept, home, mid, far = backproject(grads, got, 0, 2 * n * rows, weights, splits)
    far_there = flip(far, bits[0])
    crossed_term(tie(crossed, far), None, (tokens, grads[0], me_dp))
    lent, grads, chains, first, kept, home, mid, far_there = tie_all(
        lent, grads, chains, first, kept, home, mid, far_there
    )

    crossed = swap(grads[1][0])
    mid_there = flip(mid, bits[0])
    advance(0)
    back = {across[0]: shift(total([kept[n - 1], far_there]).astype(BF16), n - across[0])}
    mine = outer(tokens, grads[1:], me_dp, share, F32)
    crossed_term(tie(crossed, mine[0]), mine[0])
    mid_there, back, home, kept, grads, mine, chains, arrived, first = tie_all(
        mid_there, back, home, kept, grads, mine, chains, arrived, first
    )

    crossed = swap(grads[2][0])
    home_there = flip(home, bits[0])
    for c in range(2):
        advance(c)
    mid_sums = [
        total([kept[1 + i], mid_there[i * rows : (i + 1) * rows]]).astype(BF16)
        for i in range(n - 2)
    ]
    split = (n - 2) // 2
    for i, d in enumerate(others[:split]):
        back[d] = shift(mid_sums[i], n - d)
    (att,) = per_group(forward_kernel, slots, (q, k, tie(v, *mid_sums)), False)
    (proj_send,) = outer(ups, [(att, 0)], 1 - me_dp, share, BF16)
    crossed_term(tie(crossed, proj_send), mine[1])
    home_there, back, kept, mid_sums, att, proj_send, chains, arrived, first = tie_all(
        home_there, back, kept, mid_sums, att, proj_send, chains, arrived, first
    )

    crossed = swap(proj_send)
    for c in range(3):
        advance(c)
    for i, d in enumerate(others[split:], split):
        back[d] = shift(mid_sums[i], n - d)
    back[0] = total([kept[0], home_there]).astype(BF16)
    (proj_mine,) = outer(ups, [(tie(att, back[0]), 0)], me_dp, share, F32)
    begin([proj_mine, crossed])
    back, chains, arrived, first = tie_all(back, chains, arrived, first)

    for c in range(4):
        advance(c)
    where = lax.rem(jnp.arange(n, dtype=jnp.int32) + me, n)
    input_grad = placed_at([back[d] for d in range(n)], where)
    input_grad, chains, arrived = tie_all(input_grad, chains, arrived)
    for _ in range(n - 3):
        for c in range(1, 4):
            advance(c)
        input_grad, chains, arrived = tie_all(input_grad, chains, arrived)
    advance(3)
    qkv_grad = ended(range(3))
    arrived[3][-1] = tie(arrived[3][-1], qkv_grad)
    return (input_grad.reshape(inputs.shape), qkv_grad, ended([3])[0])


def solution(mesh):
    placed = (
        P("dp", "ctx", "space", None),
        P("dp", "ctx", "space", None),
        P(None, None, "space"),
        P(None, "space"),
    )
    sizes = tuple(mesh.shape[a] for a in ("dp", "ctx", "space"))
    return jax.shard_map(
        functools.partial(body, sizes),
        mesh=mesh,
        in_specs=placed,
        out_specs=(
            P("dp", "ctx", "space", None),
            P(None, ("dp", "ctx"), "space"),
            P(("dp", "ctx"), "space"),
        ),
        check_vma=False,
    )
```

```python
import functools
import math

import jax
import jax.numpy as jnp
from jax import lax
from jax.experimental import pallas as pl
from jax.experimental.pallas import tpu as pltpu
from jax.sharding import PartitionSpec as P

HS = 128
F32 = jnp.float32
BF16 = jnp.bfloat16
SCALE = 1.0 / math.sqrt(HS)


FREE = pl.CostEstimate(flops=1, bytes_accessed=1, transcendentals=0)
MIB = 1024 * 1024


def softmax_row(q, keys):
    scores = [jnp.sum(q * k, axis=-1, keepdims=True) * SCALE for k in keys]
    top = functools.reduce(jnp.maximum, scores)
    expo = [jnp.exp(s - top) for s in scores]
    total = functools.reduce(jnp.add, expo)
    return [e / total for e in expo]


def weighted(weights, values):
    return functools.reduce(jnp.add, [w * v for w, v in zip(weights, values)])


def rounded(values):
    return [v.astype(BF16).astype(F32) for v in values]


def forward_kernel(frames, heads, slot_ref, q_ref, k_ref, v_ref, att_ref):
    slots = [slot_ref[f] for f in range(frames)]
    for h in range(heads):
        cols = pl.ds(h * HS, HS)
        q, k, v = (
            [ref[0, slots[f], :, cols].astype(F32) for f in range(frames)]
            for ref in (q_ref, k_ref, v_ref)
        )
        for f in range(frames):
            probs_b = rounded(softmax_row(q[f], k[: f + 1]))
            att_ref[0, slots[f], :, cols] = weighted(probs_b, v).astype(BF16)


def backward_kernel(frames, heads, slot_ref, q_ref, k_ref, v_ref, near_ref, far_ref, dq_ref, dk_ref, dv_ref, give_ref):
    slots = [slot_ref[f] for f in range(frames)]
    for h in range(heads):
        cols = pl.ds(h * HS, HS)
        q, k, v = (
            [ref[0, slots[f], :, cols].astype(F32) for f in range(frames)]
            for ref in (q_ref, k_ref, v_ref)
        )
        far = far_ref[0, 0, :, cols].astype(F32)
        o = [
            jnp.where(
                slots[f] == frames - 1,
                far,
                near_ref[0, jnp.minimum(slots[f], frames - 2), :, cols].astype(F32),
            )
            for f in range(frames)
        ]
        dk = [None] * frames
        dv = [None] * frames
        for f in range(frames):
            probs = softmax_row(q[f], k[: f + 1])
            probs_b = rounded(probs)
            dprobs = [jnp.sum(o[f] * v[g], axis=-1, keepdims=True) for g in range(f + 1)]
            inner = weighted(probs, dprobs)
            dscores = rounded([p * (d - inner) for p, d in zip(probs, dprobs)])
            dq = weighted(dscores, k)
            dq_ref[0, slots[f], :, cols] = give_ref[0, 0, slots[f], :, cols] = (dq * SCALE).astype(BF16)
            for g in range(f + 1):
                add_k, add_v = dscores[g] * q[f], probs_b[g] * o[f]
                dk[g] = add_k if dk[g] is None else dk[g] + add_k
                dv[g] = add_v if dv[g] is None else dv[g] + add_v
        for g in range(frames):
            dk_ref[0, slots[g], :, cols] = give_ref[1, 0, slots[g], :, cols] = (dk[g] * SCALE).astype(BF16)
            dv_ref[0, slots[g], :, cols] = give_ref[2, 0, slots[g], :, cols] = dv[g].astype(BF16)


def per_group(kernel, slots, args, backward):
    groups, frames, patches, width = args[0].shape
    def block(shape):
        return pl.BlockSpec((1,) + shape[1:], lambda i, slot_ref: (i, 0, 0, 0))

    out = jax.ShapeDtypeStruct(args[0].shape, BF16)
    count = 3 if backward else 1
    outs, specs = [out] * count, [block(out.shape)] * count
    if backward:
        half = groups // 2
        outs.append(jax.ShapeDtypeStruct((3, half) + out.shape[1:], BF16))
        specs.append(
            pl.BlockSpec(
                (3, 1) + out.shape[1:], lambda i, slot_ref: (0, jnp.maximum(i - half, 0), 0, 0, 0)
            )
        )
    return pl.pallas_call(
        functools.partial(kernel, frames, width // HS),
        grid_spec=pltpu.PrefetchScalarGridSpec(
            num_scalar_prefetch=1,
            grid=(groups,),
            in_specs=[block(a.shape) for a in args],
            out_specs=specs,
        ),
        out_shape=outs,
        compiler_params=pltpu.CompilerParams(vmem_limit_bytes=12 * MIB),
        cost_estimate=FREE,
    )(slots, *args)


def mxu(a, b, contract):
    return lax.dot_general(a, b, ((contract[:1], contract[1:]), ((), ())), preferred_element_type=F32)


def block_of(extent, most):
    size = most - most % 128
    while extent % size:
        size -= 128
    return size


def in_order(sets):
    pieces = []
    for e in range(len(sets[0])):
        for held in sets:
            array, block = held[e]
            size = array.shape[1] * array.shape[2]
            pieces.append((array.reshape(-1, array.shape[-1]), size, block))
    return pieces


def project(sets, weights, grant=28):
    pieces = in_order(sets)
    count, model, width = weights.shape
    total = sum(size for _, size, _ in pieces)

    def kernel(*refs):
        x_refs, w_ref, x_ref = refs[: len(pieces)], refs[len(pieces)], refs[-1]
        step = pl.program_id(0)

        @pl.when(step == 0)
        def _():
            row = 0
            for ref, (_, size, _) in zip(x_refs, pieces):
                x_ref[row : row + size] = ref[...]
                row += size

        product = mxu(x_ref[...], w_ref[0], (1, 0)).astype(BF16)
        for s, out_ref in enumerate(refs[len(pieces) + 1 : -1]):

            @pl.when(step == s)
            def _():
                out_ref[...] = product

    out = jax.ShapeDtypeStruct((total, width), BF16)
    outs = pl.pallas_call(
        kernel,
        grid=(count,),
        in_specs=[
            pl.BlockSpec((size, model), lambda i, at=at: (at, 0), pipeline_mode=pl.Buffered(1))
            for _, size, at in pieces
        ]
        + [pl.BlockSpec((1, model, width), lambda i: (i, 0, 0))],
        out_specs=[pl.BlockSpec(out.shape, lambda i: (0, 0))] * count,
        out_shape=[out] * count,
        scratch_shapes=[pltpu.VMEM((total, model), BF16)],
        compiler_params=pltpu.CompilerParams(vmem_limit_bytes=grant * MIB),
        cost_estimate=FREE,
    )(*[array for array, _, _ in pieces], weights)
    rows = sets[0][0][0].shape[2]
    return [o.reshape(len(sets[0]), -1, rows, width) for o in outs]


def outer(sets, grads, column, share, dtype, plus=None, window=None, also=None):
    pieces = in_order(sets)
    more = in_order(also[0]) if also else []
    width = grads[0][0].shape[-1]
    count = len(grads)
    tall = sum(size for _, size, _ in pieces)
    wide = block_of(share, 768)
    steps = share // wide
    extra = [] if plus is None else [plus]
    shards, start = window or (1, 0)
    high = share // shards
    inside = wide // high

    def kernel(scalars_ref, *refs):
        x = jnp.concatenate([ref[...] for ref in refs[: len(pieces)]], 0)
        refs = refs[len(pieces) :]
        if also:
            x_more = jnp.concatenate([ref[...] for ref in refs[: len(more)]], 0)
            more_ref, refs = refs[len(more)], refs[len(more) + 1 :]
        grad_refs, out_refs = refs[:count], refs[count + len(extra) :]
        for grad_ref, out_ref in zip(grad_refs, out_refs):
            total = mxu(x, grad_ref[...], (0, 0))
            if also:
                total = total + mxu(x_more, more_ref[...], (0, 0))
            if extra:
                total = total + refs[count][...]
            total = total.astype(dtype)
            out_ref[...] = total
            if window:
                for j in range(inside):
                    at = pl.program_id(0) * inside + j - scalars_ref[1]

                    @pl.when((at >= 0) & (at < shards - 1))
                    def _():
                        out_refs[1][at] = total[j * high : (j + 1) * high]

    out = jax.ShapeDtypeStruct((share, width), dtype)
    tile = pl.BlockSpec((wide, width), lambda i, c: (i, 0))
    outs, specs = [out] * count, [tile] * count
    if window:
        outs.append(jax.ShapeDtypeStruct((shards - 1, high, width), dtype))
        specs.append(pl.BlockSpec(outs[-1].shape, lambda i, c: (0, 0, 0)))
    return pl.pallas_call(
        kernel,
        grid_spec=pltpu.PrefetchScalarGridSpec(
            num_scalar_prefetch=1,
            grid=(steps,),
            in_specs=[
                pl.BlockSpec((size, wide), lambda i, c, at=at: (at, c[0] * steps + i))
                for _, size, at in pieces
            ]
            + [
                pl.BlockSpec((size, wide), lambda i, c, at=at: (at, c[2] * steps + i))
                for _, size, at in more
            ]
            + [pl.BlockSpec((tall, width), lambda i, c: (also[1][1], 0))] * bool(also)
            + [pl.BlockSpec((tall, width), lambda i, c, at=at: (at, 0)) for _, at in grads]
            + [tile] * len(extra),
            out_specs=specs,
        ),
        out_shape=outs,
        compiler_params=pltpu.CompilerParams(vmem_limit_bytes=58 * MIB),
        cost_estimate=FREE,
    )(
        jnp.stack([jnp.asarray(x, jnp.int32) for x in (column, start, also[2] if also else 0)]),
        *[array for array, _, _ in pieces],
        *[array for array, _, _ in more],
        *([also[1][0].reshape(-1, width)] if also else []),
        *[g.reshape(-1, width) for g, _ in grads],
        *extra,
    )


def backproject(grads, more, block, rows, weights, splits):
    count, model, width = weights[0].shape
    wide = block_of(model, 512)
    halves = more.size // (count * width * rows) * 2

    def kernel(*refs):
        more_ref, w_refs, out_refs = refs[count], refs[count + 1 : count + 3], refs[count + 3 :]
        total = sum(
            mxu(refs[s][...], w_refs[0][s], (1, 1)) + mxu(more_ref[s], w_refs[1][s], (1, 1))
            for s in range(count)
        )
        row = 0
        for size, out_ref in zip(splits, out_refs):
            out_ref[...] = total[row : row + size].astype(BF16)
            row += size

    return pl.pallas_call(
        kernel,
        grid=(model // wide,),
        in_specs=[pl.BlockSpec((rows, width), lambda i, at=at: (halves * at + block, 0)) for _, at in grads]
        + [pl.BlockSpec((count, rows, width), lambda i: (0, block, 0))]
        + [pl.BlockSpec((count, wide, width), lambda i: (0, i, 0))] * 2,
        out_specs=[pl.BlockSpec((size, wide), lambda i: (0, i)) for size in splits],
        out_shape=[jax.ShapeDtypeStruct((size, model), BF16) for size in splits],
        compiler_params=pltpu.CompilerParams(vmem_limit_bytes=58 * MIB),
        cost_estimate=FREE,
    )(*[g.reshape(-1, width) for g, _ in grads], more.reshape(count, -1, width), *weights)


def placed_at(pieces, where):
    shape = pieces[0].shape
    count = len(pieces)

    def kernel(where_ref, *refs):
        for i in range(count):

            @pl.when(pl.program_id(0) == i)
            def _():
                refs[-1][0] = refs[i][...]

    return pl.pallas_call(
        kernel,
        grid_spec=pltpu.PrefetchScalarGridSpec(
            num_scalar_prefetch=1,
            grid=(count,),
            in_specs=[pl.BlockSpec(shape, lambda i, w: (0, 0))] * count,
            out_specs=pl.BlockSpec((1,) + shape, lambda i, w: (w[i], 0, 0)),
        ),
        out_shape=jax.ShapeDtypeStruct((count,) + shape, pieces[0].dtype),
        compiler_params=pltpu.CompilerParams(vmem_limit_bytes=6 * MIB),
        cost_estimate=FREE,
    )(where, *pieces)


def finished(chains, at, counts):
    arrays = [x for chain in chains for x in chain]
    _, rows, width = arrays[0].shape

    def kernel(at_ref, *refs):
        out_refs = [(ref, j) for ref, count in zip(refs[len(arrays) :], counts) for j in range(count)]
        i = 0
        for (out_ref, j), chain in zip(out_refs, chains):
            out_ref[j] = sum(ref[0].astype(F32) for ref in refs[i : i + len(chain)])
            i += len(chain)

    shapes = [(count, rows, width) for count in counts]
    return pl.pallas_call(
        kernel,
        grid_spec=pltpu.PrefetchScalarGridSpec(
            num_scalar_prefetch=1,
            grid=(1,),
            in_specs=[
                pl.BlockSpec((1, rows, width), lambda i, at_ref, j=j: (at_ref[j], 0, 0))
                for j in range(len(arrays))
            ],
            out_specs=[pl.BlockSpec(shape, lambda i, at_ref: (0, 0, 0)) for shape in shapes],
        ),
        out_shape=[jax.ShapeDtypeStruct(shape, F32) for shape in shapes],
        compiler_params=pltpu.CompilerParams(vmem_limit_bytes=60 * MIB),
        cost_estimate=FREE,
    )(jnp.stack(at).astype(jnp.int32), *arrays)


def tie(x, *first):
    return lax.optimization_barrier((x, *first))[0]


def paced(x):
    mark = pl.pallas_call(
        lambda x_ref, out_ref: out_ref.__setitem__(..., jnp.zeros_like(out_ref)),
        grid=(1,),
        in_specs=[pl.BlockSpec((1, 16, 128), lambda i: (0, 0, 0))],
        out_specs=pl.BlockSpec((8, 128), lambda i: (0, 0)),
        out_shape=jax.ShapeDtypeStruct((8, 128), F32),
        cost_estimate=pl.CostEstimate(flops=100 * 10**9, bytes_accessed=1, transcendentals=0),
    )(x)
    return tie(x, mark)


def tie_all(*x):
    leaves, tree = jax.tree.flatten(x)
    arrays = iter(lax.optimization_barrier([y for y in leaves if not isinstance(y, int)]))
    return jax.tree.unflatten(tree, [y if isinstance(y, int) else next(arrays) for y in leaves])


def body(sizes, inputs, upstream, qkv_weight, out_weight):
    n_dp, n, n_space = sizes
    me = lax.axis_index("ctx")
    me_dp = lax.axis_index("dp")
    clips, single, patches, model = inputs.shape
    width = qkv_weight.shape[2]
    rows = clips * single * patches // n
    bits = [1 << i for i in range(n_space.bit_length() - 1)][::-1]
    order = [0] + [d for d in range(1, n) if d != n // 2] + [n // 2]
    place = {d: i for i, d in enumerate(order)}
    slots = jnp.array([place[d] for d in range(n)], jnp.int32)[
        lax.rem(me - jnp.arange(n) + n, n)
    ]
    home, others, across = order[:1], order[1:-1], order[-1:]

    def shift(x, d):
        return lax.ppermute(x, "ctx", [(i, (i + d) % n) for i in range(n)])

    def flip(x, bit):
        return lax.ppermute(x, "space", [(i, i ^ bit) for i in range(n_space)])

    def swap(x):
        return lax.ppermute(x, "dp", [(0, 1), (1, 0)])

    def to(x, d):
        x = x.reshape(n, rows, model)
        return lax.dynamic_index_in_dim(x, lax.rem(me + d, n), 0, keepdims=False)

    def spread(*held):
        held = list(held)
        for bit in bits[1:]:
            held = held + [flip(h, bit) for h in held]
        return [(h, block) for h in held for block in range(h.shape[0])]

    share = model // n_dp

    def lend(held):
        return swap(lax.dynamic_slice_in_dim(held, (1 - me_dp) * share, share, 3))

    def cut(x, ds):
        return [to(x, d) for d in ds]

    def moved(pieces, ds):
        return [shift(p, d) for p, d in zip(pieces, ds)]

    send_bi = cut(inputs, across)
    near_bi = moved(send_bi, across)
    later_in, later_up = tie(inputs, *send_bi), tie(upstream, *send_bi)
    here_hi, here_hu = to(later_in, 0)[None], to(later_up, 0)[None]
    send_ci, send_cu, send_bu = cut(later_in, others), cut(later_up, others), cut(later_up, across)
    there_hi, there_hu = flip(here_hi, bits[0]), flip(here_hu, bits[0])
    weights = [qkv_weight, flip(qkv_weight, bits[-1])]
    near_bi, there_hi, there_hu, weights, send_ci, send_cu, send_bu = tie_all(
        near_bi, there_hi, there_hu, weights, send_ci, send_cu, send_bu
    )

    pair_hi, pair_hu = jnp.stack([here_hi, there_hi]), jnp.stack([here_hu, there_hu])
    here_bi = jnp.stack(near_bi)
    near_ci = moved(send_ci, others)
    there_bi = flip(here_bi, bits[0])
    lent_hi = lend(pair_hi)
    all_hi = spread(pair_hi)
    near_ci, there_bi, lent_hi, all_hi, pair_hu, send_cu, send_bu = tie_all(
        near_ci, there_bi, lent_hi, all_hi, pair_hu, send_cu, send_bu
    )

    pair_bi = jnp.stack([here_bi, there_bi])
    here_ci = jnp.stack(near_ci)
    near_cu = moved(send_cu, others)
    there_ci = flip(here_ci, bits[0])
    lent_bi = lend(pair_bi)
    all_bi = spread(pair_bi)
    near_cu, there_ci, lent_bi, all_bi, pair_hu, lent_hi, send_bu = tie_all(
        near_cu, there_ci, lent_bi, all_bi, pair_hu, lent_hi, send_bu
    )

    pair_ci = jnp.stack([here_ci, there_ci])
    here_cu = jnp.stack(near_cu)
    near_bu = moved(send_bu, across)
    there_cu = flip(here_cu, bits[0])
    lent_ci = lend(pair_ci)
    all_ci = spread(pair_ci)
    tokens = [all_hi, all_ci, all_bi]
    q, k, v = project(tokens, qkv_weight)
    near_bu, there_cu, lent_ci, q, k, v, lent_hi, lent_bi, pair_hu = tie_all(
        near_bu, there_cu, lent_ci, q, k, v, lent_hi, lent_bi, pair_hu
    )

    pair_cu = jnp.stack([here_cu, there_cu])
    here_bu = jnp.stack(near_bu)
    there_bu = flip(here_bu, bits[0])
    all_hu, all_cu = spread(pair_hu), spread(pair_cu)
    here_bu = spread(here_bu[None])
    from_hi = spread(lent_hi)
    (o_near,) = project([all_hu, all_cu], out_weight[None])
    there_bu, from_hi, here_bu, o_near, all_hu, all_cu, lent_ci, lent_bi = tie_all(
        there_bu, from_hi, here_bu, o_near, all_hu, all_cu, lent_ci, lent_bi
    )

    there_bu = spread(there_bu[None])
    all_bu = [x for pair in zip(here_bu, there_bu) for x in pair]
    (o_far,) = project([all_bu], out_weight[None], 58)
    ups = [all_hu, all_cu, all_bu]
    *grads, give = per_group(backward_kernel, slots, (q, k, v, o_near, o_far), True)
    grads, give, lent_ci, lent_bi = tie_all(grads, give, lent_ci, lent_bi)

    chains, arrived, first = [], [], []

    def total(arrays):
        return sum(x.astype(F32) for x in arrays)

    def to_send(c, step):
        count = n - 1 - step
        start = jnp.where(me == step, step + 1, 0)
        terms = [lax.dynamic_slice_in_dim(t, start, count, 0) for t in chains[c]]
        if step:
            at = jnp.where(me == step, 1, 0)
            terms.append(lax.dynamic_slice_in_dim(arrived[c][-1], at, count, 0))
        return total(terms).astype(BF16)

    def begin(terms, send=None):
        chains.append([t.reshape(n, share // n, width) for t in terms])
        arrived.append([])
        first.append(to_send(len(chains) - 1, 0) if send is None else send)

    def prepare(c):
        arrived[c][-1] = tie(arrived[c][-1], chains[-1][0])
        first[c] = to_send(c, len(arrived[c]))

    def crossed_term(came, plus, also=None):
        window = (n, jnp.where(me == 0, 1, 0))
        term, send = outer(lent, [(came, 0)], 0, share, BF16, plus, window, also)
        begin([term], send)
        return term

    def advance(c):
        step = len(arrived[c])
        if step == n - 1:
            return
        send = to_send(c, step) if first[c] is None else first[c]
        first[c] = None
        came = lax.ppermute(send, "ctx", [(step, step + 1), (n - 1 - step, n - 2 - step)])
        arrived[c].append(came if step else paced(came))

    def mine_of(step):
        return jnp.where(me == step + 1, 0, n - 2 - step)

    for _ in bits[2:]:
        raise NotImplementedError
    crossed = swap(grads[0])
    got = flip(give, bits[-1])
    lent = [from_hi, spread(lent_ci), spread(lent_bi)]
    grads = [(g, 0) for g in grads]
    splits = [rows] * (n + 1) + [(n - 2) * rows, rows]
    *kept, home, mid, far = backproject(grads, got, 0, 2 * n * rows, weights, splits)
    far_there = flip(far, bits[0])
    crossed_term(tie(crossed, far), None, (tokens, grads[0], me_dp))
    lent, grads, chains, first, kept, home, mid, far_there = tie_all(
        lent, grads, chains, first, kept, home, mid, far_there
    )

    crossed = swap(grads[1][0])
    mid_there = flip(mid, bits[0])
    advance(0)
    back = {across[0]: shift(total([kept[n - 1], far_there]).astype(BF16), n - across[0])}
    mine = outer(tokens, grads[1:], me_dp, share, F32)
    crossed_term(tie(crossed, mine[0]), mine[0])
    prepare(0)
    mid_there = tie(mid_there, chains[-1][0])
    mid_sums = [
        total([kept[1 + i], mid_there[i * rows : (i + 1) * rows]]).astype(BF16)
        for i in range(n - 2)
    ]
    mid_sums, back, home, kept, grads, mine, chains, arrived, first = tie_all(
        mid_sums, back, home, kept, grads, mine, chains, arrived, first
    )

    crossed = swap(grads[2][0])
    home_there = flip(home, bits[0])
    for c in (1, 0):
        advance(c)
    split = (n - 2) // 2
    for i, d in enumerate(others[:split]):
        back[d] = shift(mid_sums[i], n - d)
    (att,) = per_group(forward_kernel, slots, (q, k, tie(v, *mid_sums)), False)
    (proj_send,) = outer(ups, [(att, 0)], 1 - me_dp, share, BF16)
    crossed_term(tie(crossed, proj_send), mine[1])
    if n > 3:
        prepare(0)
    home_there, back, kept, mid_sums, att, proj_send, chains, arrived, first = tie_all(
        home_there, back, kept, mid_sums, att, proj_send, chains, arrived, first
    )

    crossed = swap(proj_send)
    for c in (2, 1, 0):
        advance(c)
    for i, d in enumerate(others[split:], split):
        back[d] = shift(mid_sums[i], n - d)
    back[0] = total([kept[0], home_there]).astype(BF16)
    (proj_mine,) = outer(ups, [(tie(att, back[0]), 0)], me_dp, share, F32)
    begin([proj_mine, crossed])
    back, chains, arrived, first = tie_all(back, chains, arrived, first)

    for c in (3, 2, 1, 0):
        advance(c)
    where = lax.rem(jnp.arange(n, dtype=jnp.int32) + me, n)
    input_grad = placed_at([back[d] for d in range(n)], where)
    input_grad, chains, arrived = tie_all(input_grad, chains, arrived)
    for _ in range(n - 3):
        for c in (3, 2, 1):
            advance(c)
        input_grad, chains, arrived = tie_all(input_grad, chains, arrived)
    advance(3)
    arrays, at = [], []
    for c in range(4):
        came = arrived[c][: n - 1 if c < 3 else n - 2]
        arrays.append(chains[c] + came)
        at += [me] * len(chains[c]) + [mine_of(step) for step in range(len(came))]
    qkv_grad, proj_grad = finished(arrays, at, [3, 1])
    came = tie(arrived[3][-1], qkv_grad)
    proj_grad = proj_grad[0] + lax.dynamic_index_in_dim(came, mine_of(n - 2), 0, keepdims=False).astype(F32)
    return (input_grad.reshape(inputs.shape), qkv_grad, proj_grad)


def solution(mesh):
    placed = (
        P("dp", "ctx", "space", None),
        P("dp", "ctx", "space", None),
        P(None, None, "space"),
        P(None, "space"),
    )
    sizes = tuple(mesh.shape[a] for a in ("dp", "ctx", "space"))
    return jax.shard_map(
        functools.partial(body, sizes),
        mesh=mesh,
        in_specs=placed,
        out_specs=(
            P("dp", "ctx", "space", None),
            P(None, ("dp", "ctx"), "space"),
            P(("dp", "ctx"), "space"),
        ),
        check_vma=False,
    )
```

```python
import functools
import math

import jax
import jax.numpy as jnp
from jax import lax
from jax.experimental import pallas as pl
from jax.experimental.pallas import tpu as pltpu
from jax.sharding import PartitionSpec as P

HS = 128
F32 = jnp.float32
BF16 = jnp.bfloat16
SCALE = 1.0 / math.sqrt(HS)


FREE = pl.CostEstimate(flops=1, bytes_accessed=1, transcendentals=0)
MIB = 1024 * 1024


def softmax_row(q, keys):
    scores = [jnp.sum(q * k, axis=-1, keepdims=True) * SCALE for k in keys]
    top = functools.reduce(jnp.maximum, scores)
    expo = [jnp.exp(s - top) for s in scores]
    total = functools.reduce(jnp.add, expo)
    return [e / total for e in expo]


def weighted(weights, values):
    return functools.reduce(jnp.add, [w * v for w, v in zip(weights, values)])


def rounded(values):
    return [v.astype(BF16).astype(F32) for v in values]


def forward_kernel(frames, heads, slot_ref, q_ref, k_ref, v_ref, att_ref):
    slots = [slot_ref[f] for f in range(frames)]
    for h in range(heads):
        cols = pl.ds(h * HS, HS)
        q, k, v = (
            [ref[0, slots[f], :, cols].astype(F32) for f in range(frames)]
            for ref in (q_ref, k_ref, v_ref)
        )
        for f in range(frames):
            probs_b = rounded(softmax_row(q[f], k[: f + 1]))
            att_ref[0, slots[f], :, cols] = weighted(probs_b, v).astype(BF16)


def backward_kernel(frames, heads, slot_ref, q_ref, k_ref, v_ref, near_ref, far_ref, dq_ref, dk_ref, dv_ref, give_ref):
    slots = [slot_ref[f] for f in range(frames)]
    for h in range(heads):
        cols = pl.ds(h * HS, HS)
        q, k, v = (
            [ref[0, slots[f], :, cols].astype(F32) for f in range(frames)]
            for ref in (q_ref, k_ref, v_ref)
        )
        far = far_ref[0, 0, :, cols].astype(F32)
        o = [
            jnp.where(
                slots[f] == frames - 1,
                far,
                near_ref[0, jnp.minimum(slots[f], frames - 2), :, cols].astype(F32),
            )
            for f in range(frames)
        ]
        dk = [None] * frames
        dv = [None] * frames
        for f in range(frames):
            probs = softmax_row(q[f], k[: f + 1])
            probs_b = rounded(probs)
            dprobs = [jnp.sum(o[f] * v[g], axis=-1, keepdims=True) for g in range(f + 1)]
            inner = weighted(probs, dprobs)
            dscores = rounded([p * (d - inner) for p, d in zip(probs, dprobs)])
            dq = weighted(dscores, k)
            dq_ref[0, slots[f], :, cols] = give_ref[0, 0, slots[f], :, cols] = (dq * SCALE).astype(BF16)
            for g in range(f + 1):
                add_k, add_v = dscores[g] * q[f], probs_b[g] * o[f]
                dk[g] = add_k if dk[g] is None else dk[g] + add_k
                dv[g] = add_v if dv[g] is None else dv[g] + add_v
        for g in range(frames):
            dk_ref[0, slots[g], :, cols] = give_ref[1, 0, slots[g], :, cols] = (dk[g] * SCALE).astype(BF16)
            dv_ref[0, slots[g], :, cols] = give_ref[2, 0, slots[g], :, cols] = dv[g].astype(BF16)


def per_group(kernel, slots, args, backward):
    groups, frames, patches, width = args[0].shape
    def block(shape):
        return pl.BlockSpec((1,) + shape[1:], lambda i, slot_ref: (i, 0, 0, 0))

    out = jax.ShapeDtypeStruct(args[0].shape, BF16)
    count = 3 if backward else 1
    outs, specs = [out] * count, [block(out.shape)] * count
    if backward:
        half = groups // 2
        outs.append(jax.ShapeDtypeStruct((3, half) + out.shape[1:], BF16))
        specs.append(
            pl.BlockSpec(
                (3, 1) + out.shape[1:], lambda i, slot_ref: (0, jnp.maximum(i - half, 0), 0, 0, 0)
            )
        )
    return pl.pallas_call(
        functools.partial(kernel, frames, width // HS),
        grid_spec=pltpu.PrefetchScalarGridSpec(
            num_scalar_prefetch=1,
            grid=(groups,),
            in_specs=[block(a.shape) for a in args],
            out_specs=specs,
        ),
        out_shape=outs,
        compiler_params=pltpu.CompilerParams(vmem_limit_bytes=12 * MIB),
        cost_estimate=FREE,
    )(slots, *args)


def mxu(a, b, contract):
    return lax.dot_general(a, b, ((contract[:1], contract[1:]), ((), ())), preferred_element_type=F32)


def block_of(extent, most):
    size = most - most % 128
    while extent % size:
        size -= 128
    return size


def in_order(sets):
    pieces = []
    for e in range(len(sets[0])):
        for held in sets:
            array, block = held[e]
            size = array.shape[1] * array.shape[2]
            pieces.append((array.reshape(-1, array.shape[-1]), size, block))
    return pieces


def project(sets, weights, grant=28):
    pieces = in_order(sets)
    count, model, width = weights.shape
    total = sum(size for _, size, _ in pieces)

    def kernel(*refs):
        x_refs, w_ref, x_ref = refs[: len(pieces)], refs[len(pieces)], refs[-1]
        step = pl.program_id(0)

        @pl.when(step == 0)
        def _():
            row = 0
            for ref, (_, size, _) in zip(x_refs, pieces):
                x_ref[row : row + size] = ref[...]
                row += size

        product = mxu(x_ref[...], w_ref[0], (1, 0)).astype(BF16)
        for s, out_ref in enumerate(refs[len(pieces) + 1 : -1]):

            @pl.when(step == s)
            def _():
                out_ref[...] = product

    out = jax.ShapeDtypeStruct((total, width), BF16)
    outs = pl.pallas_call(
        kernel,
        grid=(count,),
        in_specs=[
            pl.BlockSpec((size, model), lambda i, at=at: (at, 0), pipeline_mode=pl.Buffered(1))
            for _, size, at in pieces
        ]
        + [pl.BlockSpec((1, model, width), lambda i: (i, 0, 0))],
        out_specs=[pl.BlockSpec(out.shape, lambda i: (0, 0))] * count,
        out_shape=[out] * count,
        scratch_shapes=[pltpu.VMEM((total, model), BF16)],
        compiler_params=pltpu.CompilerParams(vmem_limit_bytes=grant * MIB),
        cost_estimate=FREE,
    )(*[array for array, _, _ in pieces], weights)
    rows = sets[0][0][0].shape[2]
    return [o.reshape(len(sets[0]), -1, rows, width) for o in outs]


def outer(sets, grads, column, share, dtype, plus=None, window=None, also=None):
    pieces = in_order(sets)
    more = in_order(also[0]) if also else []
    width = grads[0][0].shape[-1]
    count = len(grads)
    tall = sum(size for _, size, _ in pieces)
    wide = block_of(share, 768)
    steps = share // wide
    extra = [] if plus is None else [plus]
    shards, start = window or (1, 0)
    high = share // shards
    inside = wide // high

    def kernel(scalars_ref, *refs):
        x = jnp.concatenate([ref[...] for ref in refs[: len(pieces)]], 0)
        refs = refs[len(pieces) :]
        if also:
            x_more = jnp.concatenate([ref[...] for ref in refs[: len(more)]], 0)
            more_ref, refs = refs[len(more)], refs[len(more) + 1 :]
        grad_refs, out_refs = refs[:count], refs[count + len(extra) :]
        for grad_ref, out_ref in zip(grad_refs, out_refs):
            total = mxu(x, grad_ref[...], (0, 0))
            if also:
                total = total + mxu(x_more, more_ref[...], (0, 0))
            if extra:
                total = total + refs[count][...]
            total = total.astype(dtype)
            out_ref[...] = total
            if window:
                for j in range(inside):
                    at = pl.program_id(0) * inside + j - scalars_ref[1]

                    @pl.when((at >= 0) & (at < shards - 1))
                    def _():
                        out_refs[1][at] = total[j * high : (j + 1) * high]

    out = jax.ShapeDtypeStruct((share, width), dtype)
    tile = pl.BlockSpec((wide, width), lambda i, c: (i, 0))
    outs, specs = [out] * count, [tile] * count
    if window:
        outs.append(jax.ShapeDtypeStruct((shards - 1, high, width), dtype))
        specs.append(pl.BlockSpec(outs[-1].shape, lambda i, c: (0, 0, 0)))
    return pl.pallas_call(
        kernel,
        grid_spec=pltpu.PrefetchScalarGridSpec(
            num_scalar_prefetch=1,
            grid=(steps,),
            in_specs=[
                pl.BlockSpec((size, wide), lambda i, c, at=at: (at, c[0] * steps + i))
                for _, size, at in pieces
            ]
            + [
                pl.BlockSpec((size, wide), lambda i, c, at=at: (at, c[2] * steps + i))
                for _, size, at in more
            ]
            + [pl.BlockSpec((tall, width), lambda i, c: (also[1][1], 0))] * bool(also)
            + [pl.BlockSpec((tall, width), lambda i, c, at=at: (at, 0)) for _, at in grads]
            + [tile] * len(extra),
            out_specs=specs,
        ),
        out_shape=outs,
        compiler_params=pltpu.CompilerParams(vmem_limit_bytes=58 * MIB),
        cost_estimate=FREE,
    )(
        jnp.stack([jnp.asarray(x, jnp.int32) for x in (column, start, also[2] if also else 0)]),
        *[array for array, _, _ in pieces],
        *[array for array, _, _ in more],
        *([also[1][0].reshape(-1, width)] if also else []),
        *[g.reshape(-1, width) for g, _ in grads],
        *extra,
    )


def backproject(grads, more, block, rows, weights, splits):
    count, model, width = weights[0].shape
    wide = block_of(model, 512)
    halves = more.size // (count * width * rows) * 2

    def kernel(*refs):
        more_ref, w_refs, out_refs = refs[count], refs[count + 1 : count + 3], refs[count + 3 :]
        total = sum(
            mxu(refs[s][...], w_refs[0][s], (1, 1)) + mxu(more_ref[s], w_refs[1][s], (1, 1))
            for s in range(count)
        )
        row = 0
        for size, out_ref in zip(splits, out_refs):
            out_ref[...] = total[row : row + size].astype(BF16)
            row += size

    return pl.pallas_call(
        kernel,
        grid=(model // wide,),
        in_specs=[pl.BlockSpec((rows, width), lambda i, at=at: (halves * at + block, 0)) for _, at in grads]
        + [pl.BlockSpec((count, rows, width), lambda i: (0, block, 0))]
        + [pl.BlockSpec((count, wide, width), lambda i: (0, i, 0))] * 2,
        out_specs=[pl.BlockSpec((size, wide), lambda i: (0, i)) for size in splits],
        out_shape=[jax.ShapeDtypeStruct((size, model), BF16) for size in splits],
        compiler_params=pltpu.CompilerParams(vmem_limit_bytes=58 * MIB),
        cost_estimate=FREE,
    )(*[g.reshape(-1, width) for g, _ in grads], more.reshape(count, -1, width), *weights)


def placed_at(pieces, where):
    shape = pieces[0].shape
    count = len(pieces)

    def kernel(where_ref, *refs):
        for i in range(count):

            @pl.when(pl.program_id(0) == i)
            def _():
                refs[-1][0] = refs[i][...]

    return pl.pallas_call(
        kernel,
        grid_spec=pltpu.PrefetchScalarGridSpec(
            num_scalar_prefetch=1,
            grid=(count,),
            in_specs=[pl.BlockSpec(shape, lambda i, w: (0, 0))] * count,
            out_specs=pl.BlockSpec((1,) + shape, lambda i, w: (w[i], 0, 0)),
        ),
        out_shape=jax.ShapeDtypeStruct((count,) + shape, pieces[0].dtype),
        compiler_params=pltpu.CompilerParams(vmem_limit_bytes=6 * MIB),
        cost_estimate=FREE,
    )(where, *pieces)


def finished(chains, at, counts):
    arrays = [x for chain in chains for x in chain]
    _, rows, width = arrays[0].shape

    def kernel(at_ref, *refs):
        out_refs = [(ref, j) for ref, count in zip(refs[len(arrays) :], counts) for j in range(count)]
        i = 0
        for (out_ref, j), chain in zip(out_refs, chains):
            out_ref[j] = sum(ref[0].astype(F32) for ref in refs[i : i + len(chain)])
            i += len(chain)

    shapes = [(count, rows, width) for count in counts]
    return pl.pallas_call(
        kernel,
        grid_spec=pltpu.PrefetchScalarGridSpec(
            num_scalar_prefetch=1,
            grid=(1,),
            in_specs=[
                pl.BlockSpec((1, rows, width), lambda i, at_ref, j=j: (at_ref[j], 0, 0))
                for j in range(len(arrays))
            ],
            out_specs=[pl.BlockSpec(shape, lambda i, at_ref: (0, 0, 0)) for shape in shapes],
        ),
        out_shape=[jax.ShapeDtypeStruct(shape, F32) for shape in shapes],
        compiler_params=pltpu.CompilerParams(vmem_limit_bytes=60 * MIB),
        cost_estimate=FREE,
    )(jnp.stack(at).astype(jnp.int32), *arrays)


def tie(x, *first):
    return lax.optimization_barrier((x, *first))[0]


def paced(x):
    mark = pl.pallas_call(
        lambda x_ref, out_ref: out_ref.__setitem__(..., jnp.zeros_like(out_ref)),
        grid=(1,),
        in_specs=[pl.BlockSpec((1, 16, 128), lambda i: (0, 0, 0))],
        out_specs=pl.BlockSpec((8, 128), lambda i: (0, 0)),
        out_shape=jax.ShapeDtypeStruct((8, 128), F32),
        cost_estimate=pl.CostEstimate(flops=100 * 10**9, bytes_accessed=1, transcendentals=0),
    )(x)
    return tie(x, mark)


def tie_all(*x):
    leaves, tree = jax.tree.flatten(x)
    arrays = iter(lax.optimization_barrier([y for y in leaves if not isinstance(y, int)]))
    return jax.tree.unflatten(tree, [y if isinstance(y, int) else next(arrays) for y in leaves])


def body(sizes, inputs, upstream, qkv_weight, out_weight):
    n_dp, n, n_space = sizes
    me = lax.axis_index("ctx")
    me_dp = lax.axis_index("dp")
    clips, single, patches, model = inputs.shape
    width = qkv_weight.shape[2]
    rows = clips * single * patches // n
    bits = [1 << i for i in range(n_space.bit_length() - 1)][::-1]
    order = [0] + [d for d in range(1, n) if d != n // 2] + [n // 2]
    place = {d: i for i, d in enumerate(order)}
    slots = jnp.array([place[d] for d in range(n)], jnp.int32)[
        lax.rem(me - jnp.arange(n) + n, n)
    ]
    home, others, across = order[:1], order[1:-1], order[-1:]

    def shift(x, d):
        return lax.ppermute(x, "ctx", [(i, (i + d) % n) for i in range(n)])

    def flip(x, bit):
        return lax.ppermute(x, "space", [(i, i ^ bit) for i in range(n_space)])

    def swap(x):
        return lax.ppermute(x, "dp", [(0, 1), (1, 0)])

    def to(x, d):
        x = x.reshape(n, rows, model)
        return lax.dynamic_index_in_dim(x, lax.rem(me + d, n), 0, keepdims=False)

    def spread(*held):
        held = list(held)
        for bit in bits[1:]:
            held = held + [flip(h, bit) for h in held]
        return [(h, block) for h in held for block in range(h.shape[0])]

    share = model // n_dp

    def lend(held):
        return swap(lax.dynamic_slice_in_dim(held, (1 - me_dp) * share, share, 3))

    def cut(x, ds):
        return [to(x, d) for d in ds]

    def moved(pieces, ds):
        return [shift(p, d) for p, d in zip(pieces, ds)]

    send_bi = cut(inputs, across)
    near_bi = [paced(p[None])[0] for p in moved(send_bi, across)]
    later_in, later_up = tie(inputs, *send_bi), tie(upstream, *send_bi)
    here_hi, here_hu = to(later_in, 0)[None], to(later_up, 0)[None]
    send_ci, send_cu, send_bu = cut(later_in, others), cut(later_up, others), cut(later_up, across)
    there_hi, there_hu = flip(here_hi, bits[0]), flip(here_hu, bits[0])
    weights = [qkv_weight, flip(qkv_weight, bits[-1])]
    near_bi, there_hi, there_hu, weights, send_ci, send_cu, send_bu = tie_all(
        near_bi, there_hi, there_hu, weights, send_ci, send_cu, send_bu
    )

    pair_hi, pair_hu = jnp.stack([here_hi, there_hi]), jnp.stack([here_hu, there_hu])
    here_bi = jnp.stack(near_bi)
    near_ci = moved(send_ci, others)
    there_bi = flip(here_bi, bits[0])
    lent_hi = lend(pair_hi)
    all_hi = spread(pair_hi)
    near_ci, there_bi, lent_hi, all_hi, pair_hu, send_cu, send_bu = tie_all(
        near_ci, there_bi, lent_hi, all_hi, pair_hu, send_cu, send_bu
    )

    pair_bi = jnp.stack([here_bi, there_bi])
    here_ci = jnp.stack(near_ci)
    near_cu = moved(send_cu, others)
    there_ci = flip(here_ci, bits[0])
    lent_bi = lend(pair_bi)
    all_bi = spread(pair_bi)
    near_cu, there_ci, lent_bi, all_bi, pair_hu, lent_hi, send_bu = tie_all(
        near_cu, there_ci, lent_bi, all_bi, pair_hu, lent_hi, send_bu
    )

    pair_ci = jnp.stack([here_ci, there_ci])
    here_cu = jnp.stack(near_cu)
    near_bu = moved(send_bu, across)
    there_cu = flip(here_cu, bits[0])
    lent_ci = lend(pair_ci)
    all_ci = spread(pair_ci)
    tokens = [all_hi, all_ci, all_bi]
    q, k, v = project(tokens, qkv_weight)
    near_bu, there_cu, lent_ci, q, k, v, lent_hi, lent_bi, pair_hu = tie_all(
        near_bu, there_cu, lent_ci, q, k, v, lent_hi, lent_bi, pair_hu
    )

    pair_cu = jnp.stack([here_cu, there_cu])
    here_bu = jnp.stack(near_bu)
    there_bu = flip(here_bu, bits[0])
    all_hu, all_cu = spread(pair_hu), spread(pair_cu)
    here_bu = spread(here_bu[None])
    from_hi = spread(lent_hi)
    (o_near,) = project([all_hu, all_cu], out_weight[None])
    there_bu, from_hi, here_bu, o_near, all_hu, all_cu, lent_ci, lent_bi = tie_all(
        there_bu, from_hi, here_bu, o_near, all_hu, all_cu, lent_ci, lent_bi
    )

    there_bu = spread(there_bu[None])
    all_bu = [x for pair in zip(here_bu, there_bu) for x in pair]
    (o_far,) = project([all_bu], out_weight[None], 58)
    ups = [all_hu, all_cu, all_bu]
    *grads, give = per_group(backward_kernel, slots, (q, k, v, o_near, o_far), True)
    grads, give, lent_ci, lent_bi = tie_all(grads, give, lent_ci, lent_bi)

    chains, arrived, first = [], [], []

    def total(arrays):
        return sum(x.astype(F32) for x in arrays)

    def to_send(c, step):
        count = n - 1 - step
        start = jnp.where(me == step, step + 1, 0)
        terms = [lax.dynamic_slice_in_dim(t, start, count, 0) for t in chains[c]]
        if step:
            at = jnp.where(me == step, 1, 0)
            terms.append(lax.dynamic_slice_in_dim(arrived[c][-1], at, count, 0))
        return total(terms).astype(BF16)

    def begin(terms, send=None):
        chains.append([t.reshape(n, share // n, width) for t in terms])
        arrived.append([])
        first.append(to_send(len(chains) - 1, 0) if send is None else send)

    def prepare(c):
        arrived[c][-1] = tie(arrived[c][-1], chains[-1][0])
        first[c] = to_send(c, len(arrived[c]))

    def crossed_term(came, plus, also=None):
        window = (n, jnp.where(me == 0, 1, 0))
        term, send = outer(lent, [(came, 0)], 0, share, BF16, plus, window, also)
        begin([term], send)
        return term

    def advance(c):
        step = len(arrived[c])
        if step == n - 1:
            return
        send = to_send(c, step) if first[c] is None else first[c]
        first[c] = None
        came = lax.ppermute(send, "ctx", [(step, step + 1), (n - 1 - step, n - 2 - step)])
        arrived[c].append(paced(came))

    def mine_of(step):
        return jnp.where(me == step + 1, 0, n - 2 - step)

    for _ in bits[2:]:
        raise NotImplementedError
    crossed = swap(grads[0])
    got = flip(give, bits[-1])
    lent = [from_hi, spread(lent_ci), spread(lent_bi)]
    grads = [(g, 0) for g in grads]
    splits = [rows] * (n + 1) + [(n - 2) * rows, rows]
    *kept, home, mid, far = backproject(grads, got, 0, 2 * n * rows, weights, splits)
    far_there = flip(far, bits[0])
    crossed_term(tie(crossed, far), None, (tokens, grads[0], me_dp))
    lent, grads, chains, first, kept, home, mid, far_there = tie_all(
        lent, grads, chains, first, kept, home, mid, far_there
    )

    crossed = swap(grads[1][0])
    mid_there = flip(mid, bits[0])
    advance(0)
    back = {across[0]: shift(total([kept[n - 1], far_there]).astype(BF16), n - across[0])}
    mine = outer(tokens, grads[1:], me_dp, share, F32)
    crossed_term(tie(crossed, mine[0]), mine[0])
    prepare(0)
    mid_there = tie(mid_there, chains[-1][0])
    mid_sums = [
        total([kept[1 + i], mid_there[i * rows : (i + 1) * rows]]).astype(BF16)
        for i in range(n - 2)
    ]
    mid_sums, back, home, kept, grads, mine, chains, arrived, first = tie_all(
        mid_sums, back, home, kept, grads, mine, chains, arrived, first
    )

    crossed = swap(grads[2][0])
    home_there = flip(home, bits[0])
    for c in (1, 0):
        advance(c)
    split = (n - 2) // 2
    for i, d in enumerate(others[:split]):
        back[d] = shift(mid_sums[i], n - d)
    (att,) = per_group(forward_kernel, slots, (q, k, tie(v, *mid_sums)), False)
    (proj_send,) = outer(ups, [(att, 0)], 1 - me_dp, share, BF16)
    crossed_term(tie(crossed, proj_send), mine[1])
    if n > 3:
        prepare(0)
    home_there, back, kept, mid_sums, att, proj_send, chains, arrived, first = tie_all(
        home_there, back, kept, mid_sums, att, proj_send, chains, arrived, first
    )

    crossed = swap(proj_send)
    for c in (2, 1, 0):
        advance(c)
    for i, d in enumerate(others[split:], split):
        back[d] = shift(mid_sums[i], n - d)
    back[0] = total([kept[0], home_there]).astype(BF16)
    (proj_mine,) = outer(ups, [(tie(att, back[0]), 0)], me_dp, share, F32)
    begin([proj_mine, crossed])
    back, chains, arrived, first = tie_all(back, chains, arrived, first)

    for c in (3, 2, 1, 0):
        advance(c)
    where = lax.rem(jnp.arange(n, dtype=jnp.int32) + me, n)
    input_grad = placed_at([back[d] for d in range(n)], where)
    input_grad, chains, arrived = tie_all(input_grad, chains, arrived)
    for _ in range(n - 3):
        for c in (3, 2, 1):
            advance(c)
        input_grad, chains, arrived = tie_all(input_grad, chains, arrived)
    advance(3)
    arrays, at = [], []
    for c in range(4):
        came = arrived[c][: n - 1 if c < 3 else n - 2]
        arrays.append(chains[c] + came)
        at += [me] * len(chains[c]) + [mine_of(step) for step in range(len(came))]
    qkv_grad, proj_grad = finished(arrays, at, [3, 1])
    came = tie(arrived[3][-1], qkv_grad)
    proj_grad = proj_grad[0] + lax.dynamic_index_in_dim(came, mine_of(n - 2), 0, keepdims=False).astype(F32)
    return (input_grad.reshape(inputs.shape), qkv_grad, proj_grad)


def solution(mesh):
    placed = (
        P("dp", "ctx", "space", None),
        P("dp", "ctx", "space", None),
        P(None, None, "space"),
        P(None, "space"),
    )
    sizes = tuple(mesh.shape[a] for a in ("dp", "ctx", "space"))
    return jax.shard_map(
        functools.partial(body, sizes),
        mesh=mesh,
        in_specs=placed,
        out_specs=(
            P("dp", "ctx", "space", None),
            P(None, ("dp", "ctx"), "space"),
            P(("dp", "ctx"), "space"),
        ),
        check_vma=False,
    )
```

```python
import functools
import math

import jax
import jax.numpy as jnp
from jax import lax
from jax.experimental import pallas as pl
from jax.experimental.pallas import tpu as pltpu
from jax.sharding import PartitionSpec as P

HS = 128
F32 = jnp.float32
BF16 = jnp.bfloat16
SCALE = 1.0 / math.sqrt(HS)


FREE = pl.CostEstimate(flops=1, bytes_accessed=1, transcendentals=0)
MIB = 1024 * 1024


def softmax_row(q, keys):
    scores = [jnp.sum(q * k, axis=-1, keepdims=True) * SCALE for k in keys]
    top = functools.reduce(jnp.maximum, scores)
    expo = [jnp.exp(s - top) for s in scores]
    total = functools.reduce(jnp.add, expo)
    return [e / total for e in expo]


def weighted(weights, values):
    return functools.reduce(jnp.add, [w * v for w, v in zip(weights, values)])


def rounded(values):
    return [v.astype(BF16).astype(F32) for v in values]


def forward_kernel(frames, heads, slot_ref, q_ref, k_ref, v_ref, att_ref):
    slots = [slot_ref[f] for f in range(frames)]
    for h in range(heads):
        cols = pl.ds(h * HS, HS)
        q, k, v = (
            [ref[0, slots[f], :, cols].astype(F32) for f in range(frames)]
            for ref in (q_ref, k_ref, v_ref)
        )
        for f in range(frames):
            probs_b = rounded(softmax_row(q[f], k[: f + 1]))
            att_ref[0, slots[f], :, cols] = weighted(probs_b, v).astype(BF16)


def backward_kernel(frames, heads, slot_ref, q_ref, k_ref, v_ref, near_ref, far_ref, dq_ref, dk_ref, dv_ref, give_ref):
    slots = [slot_ref[f] for f in range(frames)]
    for h in range(heads):
        cols = pl.ds(h * HS, HS)
        q, k, v = (
            [ref[0, slots[f], :, cols].astype(F32) for f in range(frames)]
            for ref in (q_ref, k_ref, v_ref)
        )
        far = far_ref[0, 0, :, cols].astype(F32)
        o = [
            jnp.where(
                slots[f] == frames - 1,
                far,
                near_ref[0, jnp.minimum(slots[f], frames - 2), :, cols].astype(F32),
            )
            for f in range(frames)
        ]
        dk = [None] * frames
        dv = [None] * frames
        for f in range(frames):
            probs = softmax_row(q[f], k[: f + 1])
            probs_b = rounded(probs)
            dprobs = [jnp.sum(o[f] * v[g], axis=-1, keepdims=True) for g in range(f + 1)]
            inner = weighted(probs, dprobs)
            dscores = rounded([p * (d - inner) for p, d in zip(probs, dprobs)])
            dq = weighted(dscores, k)
            dq_ref[0, slots[f], :, cols] = give_ref[0, 0, slots[f], :, cols] = (dq * SCALE).astype(BF16)
            for g in range(f + 1):
                add_k, add_v = dscores[g] * q[f], probs_b[g] * o[f]
                dk[g] = add_k if dk[g] is None else dk[g] + add_k
                dv[g] = add_v if dv[g] is None else dv[g] + add_v
        for g in range(frames):
            dk_ref[0, slots[g], :, cols] = give_ref[1, 0, slots[g], :, cols] = (dk[g] * SCALE).astype(BF16)
            dv_ref[0, slots[g], :, cols] = give_ref[2, 0, slots[g], :, cols] = dv[g].astype(BF16)


def per_group(kernel, slots, args, backward):
    groups, frames, patches, width = args[0].shape
    def block(shape):
        return pl.BlockSpec((1,) + shape[1:], lambda i, slot_ref: (i, 0, 0, 0))

    out = jax.ShapeDtypeStruct(args[0].shape, BF16)
    count = 3 if backward else 1
    outs, specs = [out] * count, [block(out.shape)] * count
    if backward:
        half = groups // 2
        outs.append(jax.ShapeDtypeStruct((3, half) + out.shape[1:], BF16))
        specs.append(
            pl.BlockSpec(
                (3, 1) + out.shape[1:], lambda i, slot_ref: (0, jnp.maximum(i - half, 0), 0, 0, 0)
            )
        )
    return pl.pallas_call(
        functools.partial(kernel, frames, width // HS),
        grid_spec=pltpu.PrefetchScalarGridSpec(
            num_scalar_prefetch=1,
            grid=(groups,),
            in_specs=[block(a.shape) for a in args],
            out_specs=specs,
        ),
        out_shape=outs,
        compiler_params=pltpu.CompilerParams(vmem_limit_bytes=12 * MIB),
        cost_estimate=FREE,
    )(slots, *args)


def mxu(a, b, contract):
    return lax.dot_general(a, b, ((contract[:1], contract[1:]), ((), ())), preferred_element_type=F32)


def block_of(extent, most):
    size = most - most % 128
    while extent % size:
        size -= 128
    return size


def in_order(sets):
    pieces = []
    for e in range(len(sets[0])):
        for held in sets:
            array, block = held[e]
            size = array.shape[1] * array.shape[2]
            pieces.append((array.reshape(-1, array.shape[-1]), size, block))
    return pieces


def project(sets, weights, grant=28):
    pieces = in_order(sets)
    count, model, width = weights.shape
    total = sum(size for _, size, _ in pieces)

    def kernel(*refs):
        x_refs, w_ref, x_ref = refs[: len(pieces)], refs[len(pieces)], refs[-1]
        step = pl.program_id(0)

        @pl.when(step == 0)
        def _():
            row = 0
            for ref, (_, size, _) in zip(x_refs, pieces):
                x_ref[row : row + size] = ref[...]
                row += size

        product = mxu(x_ref[...], w_ref[0], (1, 0)).astype(BF16)
        for s, out_ref in enumerate(refs[len(pieces) + 1 : -1]):

            @pl.when(step == s)
            def _():
                out_ref[...] = product

    out = jax.ShapeDtypeStruct((total, width), BF16)
    outs = pl.pallas_call(
        kernel,
        grid=(count,),
        in_specs=[
            pl.BlockSpec((size, model), lambda i, at=at: (at, 0), pipeline_mode=pl.Buffered(1))
            for _, size, at in pieces
        ]
        + [pl.BlockSpec((1, model, width), lambda i: (i, 0, 0))],
        out_specs=[pl.BlockSpec(out.shape, lambda i: (0, 0))] * count,
        out_shape=[out] * count,
        scratch_shapes=[pltpu.VMEM((total, model), BF16)],
        compiler_params=pltpu.CompilerParams(vmem_limit_bytes=grant * MIB),
        cost_estimate=FREE,
    )(*[array for array, _, _ in pieces], weights)
    rows = sets[0][0][0].shape[2]
    return [o.reshape(len(sets[0]), -1, rows, width) for o in outs]


def outer(sets, grads, column, share, dtype, plus=None, window=None, also=None):
    pieces = in_order(sets)
    more = in_order(also[0]) if also else []
    width = grads[0][0].shape[-1]
    count = len(grads)
    tall = sum(size for _, size, _ in pieces)
    wide = block_of(share, 768)
    steps = share // wide
    extra = [] if plus is None else [plus]
    shards, start = window or (1, 0)
    high = share // shards
    inside = wide // high

    def kernel(scalars_ref, *refs):
        x = jnp.concatenate([ref[...] for ref in refs[: len(pieces)]], 0)
        refs = refs[len(pieces) :]
        if also:
            x_more = jnp.concatenate([ref[...] for ref in refs[: len(more)]], 0)
            more_ref, refs = refs[len(more)], refs[len(more) + 1 :]
        grad_refs, out_refs = refs[:count], refs[count + len(extra) :]
        for grad_ref, out_ref in zip(grad_refs, out_refs):
            total = mxu(x, grad_ref[...], (0, 0))
            if also:
                total = total + mxu(x_more, more_ref[...], (0, 0))
            if extra:
                total = total + refs[count][...]
            total = total.astype(dtype)
            out_ref[...] = total
            if window:
                for j in range(inside):
                    at = pl.program_id(0) * inside + j - scalars_ref[1]

                    @pl.when((at >= 0) & (at < shards - 1))
                    def _():
                        out_refs[1][at] = total[j * high : (j + 1) * high]

    out = jax.ShapeDtypeStruct((share, width), dtype)
    tile = pl.BlockSpec((wide, width), lambda i, c: (i, 0))
    outs, specs = [out] * count, [tile] * count
    if window:
        outs.append(jax.ShapeDtypeStruct((shards - 1, high, width), dtype))
        specs.append(pl.BlockSpec(outs[-1].shape, lambda i, c: (0, 0, 0)))
    return pl.pallas_call(
        kernel,
        grid_spec=pltpu.PrefetchScalarGridSpec(
            num_scalar_prefetch=1,
            grid=(steps,),
            in_specs=[
                pl.BlockSpec((size, wide), lambda i, c, at=at: (at, c[0] * steps + i))
                for _, size, at in pieces
            ]
            + [
                pl.BlockSpec((size, wide), lambda i, c, at=at: (at, c[2] * steps + i))
                for _, size, at in more
            ]
            + [pl.BlockSpec((tall, width), lambda i, c: (also[1][1], 0))] * bool(also)
            + [pl.BlockSpec((tall, width), lambda i, c, at=at: (at, 0)) for _, at in grads]
            + [tile] * len(extra),
            out_specs=specs,
        ),
        out_shape=outs,
        compiler_params=pltpu.CompilerParams(vmem_limit_bytes=58 * MIB),
        cost_estimate=FREE,
    )(
        jnp.stack([jnp.asarray(x, jnp.int32) for x in (column, start, also[2] if also else 0)]),
        *[array for array, _, _ in pieces],
        *[array for array, _, _ in more],
        *([also[1][0].reshape(-1, width)] if also else []),
        *[g.reshape(-1, width) for g, _ in grads],
        *extra,
    )


def backproject(grads, more, block, rows, weights, splits):
    count, model, width = weights[0].shape
    wide = block_of(model, 512)
    halves = more.size // (count * width * rows) * 2

    def kernel(*refs):
        more_ref, w_refs, out_refs = refs[count], refs[count + 1 : count + 3], refs[count + 3 :]
        total = sum(
            mxu(refs[s][...], w_refs[0][s], (1, 1)) + mxu(more_ref[s], w_refs[1][s], (1, 1))
            for s in range(count)
        )
        row = 0
        for size, out_ref in zip(splits, out_refs):
            out_ref[...] = total[row : row + size].astype(BF16)
            row += size

    return pl.pallas_call(
        kernel,
        grid=(model // wide,),
        in_specs=[pl.BlockSpec((rows, width), lambda i, at=at: (halves * at + block, 0)) for _, at in grads]
        + [pl.BlockSpec((count, rows, width), lambda i: (0, block, 0))]
        + [pl.BlockSpec((count, wide, width), lambda i: (0, i, 0))] * 2,
        out_specs=[pl.BlockSpec((size, wide), lambda i: (0, i)) for size in splits],
        out_shape=[jax.ShapeDtypeStruct((size, model), BF16) for size in splits],
        compiler_params=pltpu.CompilerParams(vmem_limit_bytes=58 * MIB),
        cost_estimate=FREE,
    )(*[g.reshape(-1, width) for g, _ in grads], more.reshape(count, -1, width), *weights)


def placed_at(pieces, where):
    shape = pieces[0].shape
    count = len(pieces)

    def kernel(where_ref, *refs):
        for i in range(count):

            @pl.when(pl.program_id(0) == i)
            def _():
                refs[-1][0] = refs[i][...]

    return pl.pallas_call(
        kernel,
        grid_spec=pltpu.PrefetchScalarGridSpec(
            num_scalar_prefetch=1,
            grid=(count,),
            in_specs=[pl.BlockSpec(shape, lambda i, w: (0, 0))] * count,
            out_specs=pl.BlockSpec((1,) + shape, lambda i, w: (w[i], 0, 0)),
        ),
        out_shape=jax.ShapeDtypeStruct((count,) + shape, pieces[0].dtype),
        compiler_params=pltpu.CompilerParams(vmem_limit_bytes=6 * MIB),
        cost_estimate=FREE,
    )(where, *pieces)


def finished(chains, at, counts):
    arrays = [x for chain in chains for x in chain]
    _, rows, width = arrays[0].shape

    def kernel(at_ref, *refs):
        out_refs = [(ref, j) for ref, count in zip(refs[len(arrays) :], counts) for j in range(count)]
        i = 0
        for (out_ref, j), chain in zip(out_refs, chains):
            out_ref[j] = sum(ref[0].astype(F32) for ref in refs[i : i + len(chain)])
            i += len(chain)

    shapes = [(count, rows, width) for count in counts]
    return pl.pallas_call(
        kernel,
        grid_spec=pltpu.PrefetchScalarGridSpec(
            num_scalar_prefetch=1,
            grid=(1,),
            in_specs=[
                pl.BlockSpec((1, rows, width), lambda i, at_ref, j=j: (at_ref[j], 0, 0))
                for j in range(len(arrays))
            ],
            out_specs=[pl.BlockSpec(shape, lambda i, at_ref: (0, 0, 0)) for shape in shapes],
        ),
        out_shape=[jax.ShapeDtypeStruct(shape, F32) for shape in shapes],
        compiler_params=pltpu.CompilerParams(vmem_limit_bytes=60 * MIB),
        cost_estimate=FREE,
    )(jnp.stack(at).astype(jnp.int32), *arrays)


def tie(x, *first):
    return lax.optimization_barrier((x, *first))[0]


def paced(x):
    mark = pl.pallas_call(
        lambda x_ref, out_ref: out_ref.__setitem__(..., jnp.zeros_like(out_ref)),
        grid=(1,),
        in_specs=[pl.BlockSpec((1, 16, 128), lambda i: (0, 0, 0))],
        out_specs=pl.BlockSpec((8, 128), lambda i: (0, 0)),
        out_shape=jax.ShapeDtypeStruct((8, 128), F32),
        cost_estimate=pl.CostEstimate(flops=100 * 10**9, bytes_accessed=1, transcendentals=0),
    )(x)
    return tie(x, mark)


def tie_all(*x):
    leaves, tree = jax.tree.flatten(x)
    arrays = iter(lax.optimization_barrier([y for y in leaves if not isinstance(y, int)]))
    return jax.tree.unflatten(tree, [y if isinstance(y, int) else next(arrays) for y in leaves])


def body(sizes, inputs, upstream, qkv_weight, out_weight):
    n_dp, n, n_space = sizes
    me = lax.axis_index("ctx")
    me_dp = lax.axis_index("dp")
    clips, single, patches, model = inputs.shape
    width = qkv_weight.shape[2]
    rows = clips * single * patches // n
    bits = [1 << i for i in range(n_space.bit_length() - 1)][::-1]
    order = [0] + [d for d in range(1, n) if d != n // 2] + [n // 2]
    place = {d: i for i, d in enumerate(order)}
    slots = jnp.array([place[d] for d in range(n)], jnp.int32)[
        lax.rem(me - jnp.arange(n) + n, n)
    ]
    home, others, across = order[:1], order[1:-1], order[-1:]

    def shift(x, d):
        return lax.ppermute(x, "ctx", [(i, (i + d) % n) for i in range(n)])

    def flip(x, bit):
        return lax.ppermute(x, "space", [(i, i ^ bit) for i in range(n_space)])

    def swap(x):
        return lax.ppermute(x, "dp", [(0, 1), (1, 0)])

    def to(x, d):
        x = x.reshape(n, rows, model)
        return lax.dynamic_index_in_dim(x, lax.rem(me + d, n), 0, keepdims=False)

    def spread(*held):
        held = list(held)
        for bit in bits[1:]:
            held = held + [flip(h, bit) for h in held]
        return [(h, block) for h in held for block in range(h.shape[0])]

    share = model // n_dp

    def lend(held):
        return swap(lax.dynamic_slice_in_dim(held, (1 - me_dp) * share, share, 3))

    def cut(x, ds):
        return [to(x, d) for d in ds]

    def moved(pieces, ds):
        return [shift(p, d) for p, d in zip(pieces, ds)]

    send_bi = cut(inputs, across)
    near_bi = [paced(p[None])[0] for p in moved(send_bi, across)]
    later_in, later_up = tie(inputs, *send_bi), tie(upstream, *send_bi)
    here_hi, here_hu = to(later_in, 0)[None], to(later_up, 0)[None]
    send_ci, send_cu, send_bu = cut(later_in, others), cut(later_up, others), cut(later_up, across)
    there_hi, there_hu = flip(here_hi, bits[0]), flip(here_hu, bits[0])
    weights = [qkv_weight, flip(qkv_weight, bits[-1])]
    near_bi, there_hi, there_hu, weights, send_ci, send_cu, send_bu = tie_all(
        near_bi, there_hi, there_hu, weights, send_ci, send_cu, send_bu
    )

    pair_hi, pair_hu = jnp.stack([here_hi, there_hi]), jnp.stack([here_hu, there_hu])
    here_bi = jnp.stack(near_bi)
    near_ci = [paced(p[None])[0] for p in moved(send_ci, others)]
    there_bi = flip(here_bi, bits[0])
    lent_hi = lend(pair_hi)
    all_hi = spread(pair_hi)
    near_ci, there_bi, lent_hi, all_hi, pair_hu, send_cu, send_bu = tie_all(
        near_ci, there_bi, lent_hi, all_hi, pair_hu, send_cu, send_bu
    )

    pair_bi = jnp.stack([here_bi, there_bi])
    here_ci = jnp.stack(near_ci)
    near_cu = [paced(p[None])[0] for p in moved(send_cu, others)]
    there_ci = flip(here_ci, bits[0])
    lent_bi = lend(pair_bi)
    all_bi = spread(pair_bi)
    near_cu, there_ci, lent_bi, all_bi, pair_hu, lent_hi, send_bu = tie_all(
        near_cu, there_ci, lent_bi, all_bi, pair_hu, lent_hi, send_bu
    )

    pair_ci = jnp.stack([here_ci, there_ci])
    here_cu = jnp.stack(near_cu)
    near_bu = moved(send_bu, across)
    there_cu = flip(here_cu, bits[0])
    lent_ci = lend(pair_ci)
    all_ci = spread(pair_ci)
    tokens = [all_hi, all_ci, all_bi]
    q, k, v = project(tokens, qkv_weight)
    near_bu, there_cu, lent_ci, q, k, v, lent_hi, lent_bi, pair_hu = tie_all(
        near_bu, there_cu, lent_ci, q, k, v, lent_hi, lent_bi, pair_hu
    )

    pair_cu = jnp.stack([here_cu, there_cu])
    here_bu = jnp.stack(near_bu)
    there_bu = flip(here_bu, bits[0])
    all_hu, all_cu = spread(pair_hu), spread(pair_cu)
    here_bu = spread(here_bu[None])
    from_hi = spread(lent_hi)
    (o_near,) = project([all_hu, all_cu], out_weight[None])
    there_bu, from_hi, here_bu, o_near, all_hu, all_cu, lent_ci, lent_bi = tie_all(
        there_bu, from_hi, here_bu, o_near, all_hu, all_cu, lent_ci, lent_bi
    )

    there_bu = spread(there_bu[None])
    all_bu = [x for pair in zip(here_bu, there_bu) for x in pair]
    (o_far,) = project([all_bu], out_weight[None], 58)
    ups = [all_hu, all_cu, all_bu]
    *grads, give = per_group(backward_kernel, slots, (q, k, v, o_near, o_far), True)
    grads, give, lent_ci, lent_bi = tie_all(grads, give, lent_ci, lent_bi)

    chains, arrived, first = [], [], []

    def total(arrays):
        return sum(x.astype(F32) for x in arrays)

    def to_send(c, step):
        count = n - 1 - step
        start = jnp.where(me == step, step + 1, 0)
        terms = [lax.dynamic_slice_in_dim(t, start, count, 0) for t in chains[c]]
        if step:
            at = jnp.where(me == step, 1, 0)
            terms.append(lax.dynamic_slice_in_dim(arrived[c][-1], at, count, 0))
        return total(terms).astype(BF16)

    def begin(terms, send=None):
        chains.append([t.reshape(n, share // n, width) for t in terms])
        arrived.append([])
        first.append(to_send(len(chains) - 1, 0) if send is None else send)

    def prepare(c):
        arrived[c][-1] = tie(arrived[c][-1], chains[-1][0])
        first[c] = to_send(c, len(arrived[c]))

    def crossed_term(came, plus, also=None):
        window = (n, jnp.where(me == 0, 1, 0))
        term, send = outer(lent, [(came, 0)], 0, share, BF16, plus, window, also)
        begin([term], send)
        return term

    def advance(c):
        step = len(arrived[c])
        if step == n - 1:
            return
        send = to_send(c, step) if first[c] is None else first[c]
        first[c] = None
        came = lax.ppermute(send, "ctx", [(step, step + 1), (n - 1 - step, n - 2 - step)])
        arrived[c].append(paced(came))

    def mine_of(step):
        return jnp.where(me == step + 1, 0, n - 2 - step)

    for _ in bits[2:]:
        raise NotImplementedError
    crossed = swap(grads[0])
    got = flip(give, bits[-1])
    lent = [from_hi, spread(lent_ci), spread(lent_bi)]
    grads = [(g, 0) for g in grads]
    splits = [rows] * (n + 1) + [(n - 2) * rows, rows]
    *kept, home, mid, far = backproject(grads, got, 0, 2 * n * rows, weights, splits)
    far_there = flip(far, bits[0])
    crossed_term(tie(crossed, far), None, (tokens, grads[0], me_dp))
    lent, grads, chains, first, kept, home, mid, far_there = tie_all(
        lent, grads, chains, first, kept, home, mid, far_there
    )

    crossed = swap(grads[1][0])
    mid_there = flip(mid, bits[0])
    advance(0)
    back = {across[0]: shift(total([kept[n - 1], far_there]).astype(BF16), n - across[0])}
    mine = outer(tokens, grads[1:], me_dp, share, F32)
    crossed_term(tie(crossed, mine[0]), mine[0])
    prepare(0)
    mid_there = tie(mid_there, chains[-1][0])
    mid_sums = [
        total([kept[1 + i], mid_there[i * rows : (i + 1) * rows]]).astype(BF16)
        for i in range(n - 2)
    ]
    mid_sums, back, home, kept, grads, mine, chains, arrived, first = tie_all(
        mid_sums, back, home, kept, grads, mine, chains, arrived, first
    )

    crossed = swap(grads[2][0])
    home_there = flip(home, bits[0])
    for c in (1, 0):
        advance(c)
    split = (n - 2) // 2
    for i, d in enumerate(others[:split]):
        back[d] = shift(mid_sums[i], n - d)
    (att,) = per_group(forward_kernel, slots, (q, k, tie(v, *mid_sums)), False)
    (proj_send,) = outer(ups, [(att, 0)], 1 - me_dp, share, BF16)
    crossed_term(tie(crossed, proj_send), mine[1])
    if n > 3:
        prepare(0)
    home_there, back, kept, mid_sums, att, proj_send, chains, arrived, first = tie_all(
        home_there, back, kept, mid_sums, att, proj_send, chains, arrived, first
    )

    crossed = swap(proj_send)
    for c in (2, 1, 0):
        advance(c)
    for i, d in enumerate(others[split:], split):
        back[d] = shift(mid_sums[i], n - d)
    back[0] = total([kept[0], home_there]).astype(BF16)
    (proj_mine,) = outer(ups, [(tie(att, back[0]), 0)], me_dp, share, F32)
    begin([proj_mine, crossed])
    back, chains, arrived, first = tie_all(back, chains, arrived, first)

    for c in (3, 2, 1, 0):
        advance(c)
    where = lax.rem(jnp.arange(n, dtype=jnp.int32) + me, n)
    input_grad = placed_at([back[d] for d in range(n)], where)
    input_grad, chains, arrived = tie_all(input_grad, chains, arrived)
    for _ in range(n - 3):
        for c in (3, 2, 1):
            advance(c)
        input_grad, chains, arrived = tie_all(input_grad, chains, arrived)
    advance(3)
    arrays, at = [], []
    for c in range(4):
        came = arrived[c][: n - 1 if c < 3 else n - 2]
        arrays.append(chains[c] + came)
        at += [me] * len(chains[c]) + [mine_of(step) for step in range(len(came))]
    qkv_grad, proj_grad = finished(arrays, at, [3, 1])
    came = tie(arrived[3][-1], qkv_grad)
    proj_grad = proj_grad[0] + lax.dynamic_index_in_dim(came, mine_of(n - 2), 0, keepdims=False).astype(F32)
    return (input_grad.reshape(inputs.shape), qkv_grad, proj_grad)


def solution(mesh):
    placed = (
        P("dp", "ctx", "space", None),
        P("dp", "ctx", "space", None),
        P(None, None, "space"),
        P(None, "space"),
    )
    sizes = tuple(mesh.shape[a] for a in ("dp", "ctx", "space"))
    return jax.shard_map(
        functools.partial(body, sizes),
        mesh=mesh,
        in_specs=placed,
        out_specs=(
            P("dp", "ctx", "space", None),
            P(None, ("dp", "ctx"), "space"),
            P(("dp", "ctx"), "space"),
        ),
        check_vma=False,
    )
```

```python
import functools
import math

import jax
import jax.numpy as jnp
from jax import lax
from jax.experimental import pallas as pl
from jax.experimental.pallas import tpu as pltpu
from jax.sharding import PartitionSpec as P

HS = 128
F32 = jnp.float32
BF16 = jnp.bfloat16
SCALE = 1.0 / math.sqrt(HS)


FREE = pl.CostEstimate(flops=1, bytes_accessed=1, transcendentals=0)
MIB = 1024 * 1024


def softmax_row(q, keys):
    scores = [jnp.sum(q * k, axis=-1, keepdims=True) * SCALE for k in keys]
    top = functools.reduce(jnp.maximum, scores)
    expo = [jnp.exp(s - top) for s in scores]
    total = functools.reduce(jnp.add, expo)
    return [e / total for e in expo]


def weighted(weights, values):
    return functools.reduce(jnp.add, [w * v for w, v in zip(weights, values)])


def rounded(values):
    return [v.astype(BF16).astype(F32) for v in values]


def forward_kernel(frames, heads, slot_ref, q_ref, k_ref, v_ref, att_ref):
    slots = [slot_ref[f] for f in range(frames)]
    for h in range(heads):
        cols = pl.ds(h * HS, HS)
        q, k, v = (
            [ref[0, slots[f], :, cols].astype(F32) for f in range(frames)]
            for ref in (q_ref, k_ref, v_ref)
        )
        for f in range(frames):
            probs_b = rounded(softmax_row(q[f], k[: f + 1]))
            att_ref[0, slots[f], :, cols] = weighted(probs_b, v).astype(BF16)


def backward_kernel(frames, heads, slot_ref, q_ref, k_ref, v_ref, near_ref, far_ref, dq_ref, dk_ref, dv_ref, give_ref):
    slots = [slot_ref[f] for f in range(frames)]
    for h in range(heads):
        cols = pl.ds(h * HS, HS)
        q, k, v = (
            [ref[0, slots[f], :, cols].astype(F32) for f in range(frames)]
            for ref in (q_ref, k_ref, v_ref)
        )
        far = far_ref[0, 0, :, cols].astype(F32)
        o = [
            jnp.where(
                slots[f] == frames - 1,
                far,
                near_ref[0, jnp.minimum(slots[f], frames - 2), :, cols].astype(F32),
            )
            for f in range(frames)
        ]
        dk = [None] * frames
        dv = [None] * frames
        for f in range(frames):
            probs = softmax_row(q[f], k[: f + 1])
            probs_b = rounded(probs)
            dprobs = [jnp.sum(o[f] * v[g], axis=-1, keepdims=True) for g in range(f + 1)]
            inner = weighted(probs, dprobs)
            dscores = rounded([p * (d - inner) for p, d in zip(probs, dprobs)])
            dq = weighted(dscores, k)
            dq_ref[0, slots[f], :, cols] = give_ref[0, 0, slots[f], :, cols] = (dq * SCALE).astype(BF16)
            for g in range(f + 1):
                add_k, add_v = dscores[g] * q[f], probs_b[g] * o[f]
                dk[g] = add_k if dk[g] is None else dk[g] + add_k
                dv[g] = add_v if dv[g] is None else dv[g] + add_v
        for g in range(frames):
            dk_ref[0, slots[g], :, cols] = give_ref[1, 0, slots[g], :, cols] = (dk[g] * SCALE).astype(BF16)
            dv_ref[0, slots[g], :, cols] = give_ref[2, 0, slots[g], :, cols] = dv[g].astype(BF16)


def per_group(kernel, slots, args, backward):
    groups, frames, patches, width = args[0].shape
    def block(shape):
        return pl.BlockSpec((1,) + shape[1:], lambda i, slot_ref: (i, 0, 0, 0))

    out = jax.ShapeDtypeStruct(args[0].shape, BF16)
    count = 3 if backward else 1
    outs, specs = [out] * count, [block(out.shape)] * count
    if backward:
        half = groups // 2
        outs.append(jax.ShapeDtypeStruct((3, half) + out.shape[1:], BF16))
        specs.append(
            pl.BlockSpec(
                (3, 1) + out.shape[1:], lambda i, slot_ref: (0, jnp.maximum(i - half, 0), 0, 0, 0)
            )
        )
    return pl.pallas_call(
        functools.partial(kernel, frames, width // HS),
        grid_spec=pltpu.PrefetchScalarGridSpec(
            num_scalar_prefetch=1,
            grid=(groups,),
            in_specs=[block(a.shape) for a in args],
            out_specs=specs,
        ),
        out_shape=outs,
        compiler_params=pltpu.CompilerParams(vmem_limit_bytes=12 * MIB),
        cost_estimate=FREE,
    )(slots, *args)


def mxu(a, b, contract):
    return lax.dot_general(a, b, ((contract[:1], contract[1:]), ((), ())), preferred_element_type=F32)


def block_of(extent, most):
    size = most - most % 128
    while extent % size:
        size -= 128
    return size


def in_order(sets):
    pieces = []
    for e in range(len(sets[0])):
        for held in sets:
            array, block = held[e]
            size = array.shape[1] * array.shape[2]
            pieces.append((array.reshape(-1, array.shape[-1]), size, block))
    return pieces


def project(sets, weights, grant=28):
    pieces = in_order(sets)
    count, model, width = weights.shape
    total = sum(size for _, size, _ in pieces)

    def kernel(*refs):
        x_refs, w_ref, x_ref = refs[: len(pieces)], refs[len(pieces)], refs[-1]
        step = pl.program_id(0)

        @pl.when(step == 0)
        def _():
            row = 0
            for ref, (_, size, _) in zip(x_refs, pieces):
                x_ref[row : row + size] = ref[...]
                row += size

        product = mxu(x_ref[...], w_ref[0], (1, 0)).astype(BF16)
        for s, out_ref in enumerate(refs[len(pieces) + 1 : -1]):

            @pl.when(step == s)
            def _():
                out_ref[...] = product

    out = jax.ShapeDtypeStruct((total, width), BF16)
    outs = pl.pallas_call(
        kernel,
        grid=(count,),
        in_specs=[
            pl.BlockSpec((size, model), lambda i, at=at: (at, 0), pipeline_mode=pl.Buffered(1))
            for _, size, at in pieces
        ]
        + [pl.BlockSpec((1, model, width), lambda i: (i, 0, 0))],
        out_specs=[pl.BlockSpec(out.shape, lambda i: (0, 0))] * count,
        out_shape=[out] * count,
        scratch_shapes=[pltpu.VMEM((total, model), BF16)],
        compiler_params=pltpu.CompilerParams(vmem_limit_bytes=grant * MIB),
        cost_estimate=FREE,
    )(*[array for array, _, _ in pieces], weights)
    rows = sets[0][0][0].shape[2]
    return [o.reshape(len(sets[0]), -1, rows, width) for o in outs]


def outer(sets, grads, column, share, dtype, plus=None, window=None, also=None):
    pieces = in_order(sets)
    more = in_order(also[0]) if also else []
    width = grads[0][0].shape[-1]
    count = len(grads)
    tall = sum(size for _, size, _ in pieces)
    wide = block_of(share, 768)
    steps = share // wide
    extra = [] if plus is None else [plus]
    shards, start = window or (1, 0)
    high = share // shards
    inside = wide // high

    def kernel(scalars_ref, *refs):
        x = jnp.concatenate([ref[...] for ref in refs[: len(pieces)]], 0)
        refs = refs[len(pieces) :]
        if also:
            x_more = jnp.concatenate([ref[...] for ref in refs[: len(more)]], 0)
            more_ref, refs = refs[len(more)], refs[len(more) + 1 :]
        grad_refs, out_refs = refs[:count], refs[count + len(extra) :]
        for grad_ref, out_ref in zip(grad_refs, out_refs):
            total = mxu(x, grad_ref[...], (0, 0))
            if also:
                total = total + mxu(x_more, more_ref[...], (0, 0))
            if extra:
                total = total + refs[count][...]
            total = total.astype(dtype)
            out_ref[...] = total
            if window:
                for j in range(inside):
                    at = pl.program_id(0) * inside + j - scalars_ref[1]

                    @pl.when((at >= 0) & (at < shards - 1))
                    def _():
                        out_refs[1][at] = total[j * high : (j + 1) * high]

    out = jax.ShapeDtypeStruct((share, width), dtype)
    tile = pl.BlockSpec((wide, width), lambda i, c: (i, 0))
    outs, specs = [out] * count, [tile] * count
    if window:
        outs.append(jax.ShapeDtypeStruct((shards - 1, high, width), dtype))
        specs.append(pl.BlockSpec(outs[-1].shape, lambda i, c: (0, 0, 0)))
    return pl.pallas_call(
        kernel,
        grid_spec=pltpu.PrefetchScalarGridSpec(
            num_scalar_prefetch=1,
            grid=(steps,),
            in_specs=[
                pl.BlockSpec((size, wide), lambda i, c, at=at: (at, c[0] * steps + i))
                for _, size, at in pieces
            ]
            + [
                pl.BlockSpec((size, wide), lambda i, c, at=at: (at, c[2] * steps + i))
                for _, size, at in more
            ]
            + [pl.BlockSpec((tall, width), lambda i, c: (also[1][1], 0))] * bool(also)
            + [pl.BlockSpec((tall, width), lambda i, c, at=at: (at, 0)) for _, at in grads]
            + [tile] * len(extra),
            out_specs=specs,
        ),
        out_shape=outs,
        compiler_params=pltpu.CompilerParams(vmem_limit_bytes=58 * MIB),
        cost_estimate=FREE,
    )(
        jnp.stack([jnp.asarray(x, jnp.int32) for x in (column, start, also[2] if also else 0)]),
        *[array for array, _, _ in pieces],
        *[array for array, _, _ in more],
        *([also[1][0].reshape(-1, width)] if also else []),
        *[g.reshape(-1, width) for g, _ in grads],
        *extra,
    )


def backproject(grads, more, block, rows, weights, splits):
    count, model, width = weights[0].shape
    wide = block_of(model, 512)
    halves = more.size // (count * width * rows) * 2

    def kernel(*refs):
        more_ref, w_refs, out_refs = refs[count], refs[count + 1 : count + 3], refs[count + 3 :]
        total = sum(
            mxu(refs[s][...], w_refs[0][s], (1, 1)) + mxu(more_ref[s], w_refs[1][s], (1, 1))
            for s in range(count)
        )
        row = 0
        for size, out_ref in zip(splits, out_refs):
            out_ref[...] = total[row : row + size].astype(BF16)
            row += size

    return pl.pallas_call(
        kernel,
        grid=(model // wide,),
        in_specs=[pl.BlockSpec((rows, width), lambda i, at=at: (halves * at + block, 0)) for _, at in grads]
        + [pl.BlockSpec((count, rows, width), lambda i: (0, block, 0))]
        + [pl.BlockSpec((count, wide, width), lambda i: (0, i, 0))] * 2,
        out_specs=[pl.BlockSpec((size, wide), lambda i: (0, i)) for size in splits],
        out_shape=[jax.ShapeDtypeStruct((size, model), BF16) for size in splits],
        compiler_params=pltpu.CompilerParams(vmem_limit_bytes=58 * MIB),
        cost_estimate=FREE,
    )(*[g.reshape(-1, width) for g, _ in grads], more.reshape(count, -1, width), *weights)


def placed_at(pieces, where):
    shape = pieces[0].shape
    count = len(pieces)

    def kernel(where_ref, *refs):
        for i in range(count):

            @pl.when(pl.program_id(0) == i)
            def _():
                refs[-1][0] = refs[i][...]

    return pl.pallas_call(
        kernel,
        grid_spec=pltpu.PrefetchScalarGridSpec(
            num_scalar_prefetch=1,
            grid=(count,),
            in_specs=[pl.BlockSpec(shape, lambda i, w: (0, 0))] * count,
            out_specs=pl.BlockSpec((1,) + shape, lambda i, w: (w[i], 0, 0)),
        ),
        out_shape=jax.ShapeDtypeStruct((count,) + shape, pieces[0].dtype),
        compiler_params=pltpu.CompilerParams(vmem_limit_bytes=6 * MIB),
        cost_estimate=FREE,
    )(where, *pieces)


def finished(chains, at, counts):
    arrays = [x for chain in chains for x in chain]
    _, rows, width = arrays[0].shape

    def kernel(at_ref, *refs):
        out_refs = [(ref, j) for ref, count in zip(refs[len(arrays) :], counts) for j in range(count)]
        i = 0
        for (out_ref, j), chain in zip(out_refs, chains):
            out_ref[j] = sum(ref[0].astype(F32) for ref in refs[i : i + len(chain)])
            i += len(chain)

    shapes = [(count, rows, width) for count in counts]
    return pl.pallas_call(
        kernel,
        grid_spec=pltpu.PrefetchScalarGridSpec(
            num_scalar_prefetch=1,
            grid=(1,),
            in_specs=[
                pl.BlockSpec((1, rows, width), lambda i, at_ref, j=j: (at_ref[j], 0, 0))
                for j in range(len(arrays))
            ],
            out_specs=[pl.BlockSpec(shape, lambda i, at_ref: (0, 0, 0)) for shape in shapes],
        ),
        out_shape=[jax.ShapeDtypeStruct(shape, F32) for shape in shapes],
        compiler_params=pltpu.CompilerParams(vmem_limit_bytes=60 * MIB),
        cost_estimate=FREE,
    )(jnp.stack(at).astype(jnp.int32), *arrays)


def tie(x, *first):
    return lax.optimization_barrier((x, *first))[0]


def paced(x):
    mark = pl.pallas_call(
        lambda x_ref, out_ref: out_ref.__setitem__(..., jnp.zeros_like(out_ref)),
        grid=(1,),
        in_specs=[pl.BlockSpec((1, 16, 128), lambda i: (0, 0, 0))],
        out_specs=pl.BlockSpec((8, 128), lambda i: (0, 0)),
        out_shape=jax.ShapeDtypeStruct((8, 128), F32),
        cost_estimate=pl.CostEstimate(flops=100 * 10**9, bytes_accessed=1, transcendentals=0),
    )(x)
    return tie(x, mark)


def tie_all(*x):
    leaves, tree = jax.tree.flatten(x)
    arrays = iter(lax.optimization_barrier([y for y in leaves if not isinstance(y, int)]))
    return jax.tree.unflatten(tree, [y if isinstance(y, int) else next(arrays) for y in leaves])


def body(sizes, inputs, upstream, qkv_weight, out_weight):
    n_dp, n, n_space = sizes
    me = lax.axis_index("ctx")
    me_dp = lax.axis_index("dp")
    clips, single, patches, model = inputs.shape
    width = qkv_weight.shape[2]
    rows = clips * single * patches // n
    bits = [1 << i for i in range(n_space.bit_length() - 1)][::-1]
    order = [0] + [d for d in range(1, n) if d != n // 2] + [n // 2]
    place = {d: i for i, d in enumerate(order)}
    slots = jnp.array([place[d] for d in range(n)], jnp.int32)[
        lax.rem(me - jnp.arange(n) + n, n)
    ]
    home, others, across = order[:1], order[1:-1], order[-1:]

    def shift(x, d):
        return lax.ppermute(x, "ctx", [(i, (i + d) % n) for i in range(n)])

    def flip(x, bit):
        return lax.ppermute(x, "space", [(i, i ^ bit) for i in range(n_space)])

    def swap(x):
        return lax.ppermute(x, "dp", [(0, 1), (1, 0)])

    def to(x, d):
        x = x.reshape(n, rows, model)
        return lax.dynamic_index_in_dim(x, lax.rem(me + d, n), 0, keepdims=False)

    def spread(*held):
        held = list(held)
        for bit in bits[1:]:
            held = held + [flip(h, bit) for h in held]
        return [(h, block) for h in held for block in range(h.shape[0])]

    share = model // n_dp

    def lend(held):
        return swap(lax.dynamic_slice_in_dim(held, (1 - me_dp) * share, share, 3))

    def cut(x, ds):
        return [to(x, d) for d in ds]

    def moved(pieces, ds):
        return [shift(p, d) for p, d in zip(pieces, ds)]

    send_bi = cut(inputs, across)
    near_bi = [paced(p[None])[0] for p in moved(send_bi, across)]
    later_in, later_up = tie(inputs, *send_bi), tie(upstream, *send_bi)
    here_hi, here_hu = to(later_in, 0)[None], to(later_up, 0)[None]
    send_ci, send_cu, send_bu = cut(later_in, others), cut(later_up, others), cut(later_up, across)
    there_hi, there_hu = flip(here_hi, bits[0]), flip(here_hu, bits[0])
    weights = [qkv_weight, flip(qkv_weight, bits[-1])]
    near_bi, there_hi, there_hu, weights, send_ci, send_cu, send_bu = tie_all(
        near_bi, there_hi, there_hu, weights, send_ci, send_cu, send_bu
    )

    pair_hi, pair_hu = jnp.stack([here_hi, there_hi]), jnp.stack([here_hu, there_hu])
    here_bi = jnp.stack(near_bi)
    near_ci = [paced(p[None])[0] for p in moved(send_ci, others)]
    there_bi = flip(here_bi, bits[0])
    lent_hi = lend(pair_hi)
    all_hi = spread(pair_hi)
    near_ci, there_bi, lent_hi, all_hi, pair_hu, send_cu, send_bu = tie_all(
        near_ci, there_bi, lent_hi, all_hi, pair_hu, send_cu, send_bu
    )

    pair_bi = jnp.stack([here_bi, there_bi])
    here_ci = jnp.stack(near_ci)
    near_cu = [paced(p[None])[0] for p in moved(send_cu, others)]
    there_ci = flip(here_ci, bits[0])
    lent_bi = lend(pair_bi)
    all_bi = spread(pair_bi)
    near_cu, there_ci, lent_bi, all_bi, pair_hu, lent_hi, send_bu = tie_all(
        near_cu, there_ci, lent_bi, all_bi, pair_hu, lent_hi, send_bu
    )

    pair_ci = jnp.stack([here_ci, there_ci])
    here_cu = jnp.stack(near_cu)
    near_bu = moved(send_bu, across)
    there_cu = flip(here_cu, bits[0])
    lent_ci = lend(pair_ci)
    all_ci = spread(pair_ci)
    tokens = [all_hi, all_ci, all_bi]
    q, k, v = project(tokens, qkv_weight)
    near_bu, there_cu, lent_ci, q, k, v, lent_hi, lent_bi, pair_hu = tie_all(
        near_bu, there_cu, lent_ci, q, k, v, lent_hi, lent_bi, pair_hu
    )

    pair_cu = jnp.stack([here_cu, there_cu])
    here_bu = jnp.stack(near_bu)
    there_bu = flip(here_bu, bits[0])
    all_hu, all_cu = spread(pair_hu), spread(pair_cu)
    here_bu = spread(here_bu[None])
    from_hi = spread(lent_hi)
    (o_near,) = project([all_hu, all_cu], out_weight[None])
    there_bu = paced(tie(there_bu, o_near))
    there_bu, from_hi, here_bu, o_near, all_hu, all_cu, lent_ci, lent_bi = tie_all(
        there_bu, from_hi, here_bu, o_near, all_hu, all_cu, lent_ci, lent_bi
    )

    there_bu = spread(there_bu[None])
    all_bu = [x for pair in zip(here_bu, there_bu) for x in pair]
    (o_far,) = project([all_bu], out_weight[None], 58)
    ups = [all_hu, all_cu, all_bu]
    *grads, give = per_group(backward_kernel, slots, (q, k, v, o_near, o_far), True)
    grads, give, lent_ci, lent_bi = tie_all(grads, give, lent_ci, lent_bi)

    chains, arrived, first = [], [], []

    def total(arrays):
        return sum(x.astype(F32) for x in arrays)

    def to_send(c, step):
        count = n - 1 - step
        start = jnp.where(me == step, step + 1, 0)
        terms = [lax.dynamic_slice_in_dim(t, start, count, 0) for t in chains[c]]
        if step:
            at = jnp.where(me == step, 1, 0)
            terms.append(lax.dynamic_slice_in_dim(arrived[c][-1], at, count, 0))
        return total(terms).astype(BF16)

    def begin(terms, send=None):
        chains.append([t.reshape(n, share // n, width) for t in terms])
        arrived.append([])
        first.append(to_send(len(chains) - 1, 0) if send is None else send)

    def prepare(c):
        arrived[c][-1] = tie(arrived[c][-1], chains[-1][0])
        first[c] = to_send(c, len(arrived[c]))

    def crossed_term(came, plus, also=None):
        window = (n, jnp.where(me == 0, 1, 0))
        term, send = outer(lent, [(came, 0)], 0, share, BF16, plus, window, also)
        begin([term], send)
        return term

    def advance(c):
        step = len(arrived[c])
        if step == n - 1:
            return
        send = to_send(c, step) if first[c] is None else first[c]
        first[c] = None
        came = lax.ppermute(send, "ctx", [(step, step + 1), (n - 1 - step, n - 2 - step)])
        arrived[c].append(paced(came))

    def mine_of(step):
        return jnp.where(me == step + 1, 0, n - 2 - step)

    for _ in bits[2:]:
        raise NotImplementedError
    crossed = swap(grads[0])
    got = flip(give, bits[-1])
    lent = [from_hi, spread(lent_ci), spread(lent_bi)]
    grads = [(g, 0) for g in grads]
    splits = [rows] * (n + 1) + [(n - 2) * rows, rows]
    *kept, home, mid, far = backproject(grads, got, 0, 2 * n * rows, weights, splits)
    far_there = flip(far, bits[0])
    crossed_term(tie(crossed, far), None, (tokens, grads[0], me_dp))
    lent, grads, chains, first, kept, home, mid, far_there = tie_all(
        lent, grads, chains, first, kept, home, mid, far_there
    )

    crossed = swap(grads[1][0])
    mid_there = flip(mid, bits[0])
    advance(0)
    back = {across[0]: shift(total([kept[n - 1], far_there]).astype(BF16), n - across[0])}
    mine = outer(tokens, grads[1:], me_dp, share, F32)
    crossed_term(tie(crossed, mine[0]), mine[0])
    prepare(0)
    mid_there = tie(mid_there, chains[-1][0])
    mid_sums = [
        total([kept[1 + i], mid_there[i * rows : (i + 1) * rows]]).astype(BF16)
        for i in range(n - 2)
    ]
    mid_sums, back, home, kept, grads, mine, chains, arrived, first = tie_all(
        mid_sums, back, home, kept, grads, mine, chains, arrived, first
    )

    crossed = swap(grads[2][0])
    home_there = flip(home, bits[0])
    for c in (1, 0):
        advance(c)
    split = (n - 2) // 2
    for i, d in enumerate(others[:split]):
        back[d] = shift(mid_sums[i], n - d)
    (att,) = per_group(forward_kernel, slots, (q, k, tie(v, *mid_sums)), False)
    (proj_send,) = outer(ups, [(att, 0)], 1 - me_dp, share, BF16)
    crossed_term(tie(crossed, proj_send), mine[1])
    if n > 3:
        prepare(0)
    home_there, back, kept, mid_sums, att, proj_send, chains, arrived, first = tie_all(
        home_there, back, kept, mid_sums, att, proj_send, chains, arrived, first
    )

    crossed = swap(proj_send)
    for c in (2, 1, 0):
        advance(c)
    for i, d in enumerate(others[split:], split):
        back[d] = shift(mid_sums[i], n - d)
    back[0] = total([kept[0], home_there]).astype(BF16)
    (proj_mine,) = outer(ups, [(tie(att, back[0]), 0)], me_dp, share, F32)
    begin([proj_mine, crossed])
    back, chains, arrived, first = tie_all(back, chains, arrived, first)

    for c in (3, 2, 1, 0):
        advance(c)
    where = lax.rem(jnp.arange(n, dtype=jnp.int32) + me, n)
    input_grad = placed_at([back[d] for d in range(n)], where)
    input_grad, chains, arrived = tie_all(input_grad, chains, arrived)
    for _ in range(n - 3):
        for c in (3, 2, 1):
            advance(c)
        input_grad, chains, arrived = tie_all(input_grad, chains, arrived)
    advance(3)
    arrays, at = [], []
    for c in range(4):
        came = arrived[c][: n - 1 if c < 3 else n - 2]
        arrays.append(chains[c] + came)
        at += [me] * len(chains[c]) + [mine_of(step) for step in range(len(came))]
    qkv_grad, proj_grad = finished(arrays, at, [3, 1])
    came = tie(arrived[3][-1], qkv_grad)
    proj_grad = proj_grad[0] + lax.dynamic_index_in_dim(came, mine_of(n - 2), 0, keepdims=False).astype(F32)
    return (input_grad.reshape(inputs.shape), qkv_grad, proj_grad)


def solution(mesh):
    placed = (
        P("dp", "ctx", "space", None),
        P("dp", "ctx", "space", None),
        P(None, None, "space"),
        P(None, "space"),
    )
    sizes = tuple(mesh.shape[a] for a in ("dp", "ctx", "space"))
    return jax.shard_map(
        functools.partial(body, sizes),
        mesh=mesh,
        in_specs=placed,
        out_specs=(
            P("dp", "ctx", "space", None),
            P(None, ("dp", "ctx"), "space"),
            P(("dp", "ctx"), "space"),
        ),
        check_vma=False,
    )
```
